512 devices in a mesh: branch: 16 (over z, core), sub: 32 (over y, x).
Axes of the slice: x: 4, y: 8, z: 8, core: 2. Of those that a mesh axis runs over, the one named last changes fastest.
Arguments:
- sources: bfloat16 [64, 4194304], P(None, ('branch', 'sub')), may hold values from -6 to 6
- coords: bfloat16 [3, 4194304], P(None, ('branch', 'sub')), may hold values from 0 to 1
- leaf_basis: bfloat16 [16384, 64, 256], P(('branch', 'sub')), may hold values from -0.375 to 0.375
- leaf_transfer: float32 [16384, 64, 64], P(('branch', 'sub')), may hold values from -0.75 to 0.75
- cluster_transfer: float32 [512, 64, 64], P(('branch', 'sub'))
- near_slots: int32 [16384, 5], P(('branch', 'sub')), may hold values from 0 to 4, as said below
- near_count: int32 [16384], P(('branch', 'sub')), may hold values from 1 to 5, as said below
- cluster_partners: int32 [512, 6], P(('branch', 'sub')), may hold values from 0 to 31, as said below
- cluster_count: int32 [512], P(('branch', 'sub')), may hold values from 1 to 6, as said below
- cluster_coupling: float32 [512, 6, 64, 64], P(('branch', 'sub')), may hold values from -1.5 to 1.5
- branch_partners: int32 [16, 3], P('branch'), may hold values from 0 to 15, as said below
- branch_count: int32 [16], P('branch'), may hold values from 1 to 3, as said below
- branch_coupling_tiles: float32 [16, 3, 64, 64], P('branch'), may hold values from -1.5 to 1.5
Outputs:
- potential: float32 [64, 4194304], P(None, ('branch', 'sub'))
The draws below stay inside these ranges and needn't reach their ends.
Inputs may be any that keep to these rules, and one draw needn't show every extreme that they name: `near_slots`: entry v of leaf i's row names leaf i + v - 2; each row holds every value once. Slot 0 holds 0 on the first leaf of each device's 32, and 4 on the last one (0 where they coincide). The first near_count[i] slots of leaf i are live. On every device all leaves have 5 live slots, or all have at most 2. `cluster_partners`: A row names 6 different device clusters of the same branch, never its own. The first cluster_count[d] slots of device cluster d are live. `branch_partners`: A row names 3 different branches, never its own. The first branch_count[b] slots of branch b are live.
All inputs are finite; a program needn't handle non-finite values.
Results may differ from the reference program's by a relative error of at most 0.0028.
Values may be sent and summed in bfloat16 or wider, within the bound.
A program may use at most 64 MiB of HBM per device.

```python
import jax
import jax.numpy as jnp
from jax import lax

LEAF = 256
RANK = 64
COLS = 64
LEAF_DEV = 32
NEAR = 5
COUP = 6
BCOUP = 3
REACH = 2
LEAVES = 16384
NPTS = 4194304
N_BRANCH = 16
N_SUB = 32
DEVICES = 512


def distinct_partners(key, rows, width, picks):
    scores = jax.random.randint(key, (rows, width), 0, 65536) * width + jnp.arange(width, dtype=jnp.int32)[None, :]
    owned = (jnp.arange(rows, dtype=jnp.int32) % width)[:, None] == jnp.arange(width, dtype=jnp.int32)[None, :]
    scores = jnp.where(owned, 65536 * width + width, scores)
    return jnp.argsort(scores, axis=1, stable=True)[:, :picks].astype(jnp.int32)


def capped_counts(key, rows, most):
    first_key, second_key = jax.random.split(key)
    counts = jax.random.randint(first_key, (rows,), 1, most + 1)
    chosen = jax.random.randint(second_key, (), 0, rows)
    return jnp.where(jnp.arange(rows, dtype=jnp.int32) == chosen, most, counts).astype(jnp.int32)


def draw_cluster_transfer(key, part):
    key = jax.random.fold_in(key, 17)
    base_key, column_key = jax.random.split(key, 2)
    position = (jnp.arange(DEVICES, dtype=jnp.int32) % N_SUB).astype(jnp.float32) / max(N_SUB - 1, 1)
    rising = 0.6 * jnp.power(3.0, position)
    columns = jnp.exp(jax.random.uniform(column_key, (RANK,), minval=-1.15, maxval=1.15))
    base = jax.random.normal(base_key, (DEVICES, RANK, RANK))
    return (base * RANK ** (-0.5) * rising[:, None, None] * columns[None, None, :]).astype(jnp.float32)


def draw_near_slots(key, part):
    key = jax.random.fold_in(key, 11)
    values = jnp.arange(NEAR, dtype=jnp.int32)[None, :]
    scores = jax.random.randint(key, (LEAVES, NEAR), 0, 65536) * NEAR + values
    position = (jnp.arange(LEAVES, dtype=jnp.int32) % LEAF_DEV)[:, None]
    first_leaf = position == 0
    last_leaf = jnp.logical_and(position == LEAF_DEV - 1, jnp.logical_not(first_leaf))
    scores = jnp.where(jnp.logical_and(first_leaf, values == 0), -1, scores)
    scores = jnp.where(jnp.logical_and(last_leaf, values == NEAR - 1), -1, scores)
    return jnp.argsort(scores, axis=1, stable=True).astype(jnp.int32)


def draw_near_count(key, part):
    key = jax.random.fold_in(key, 13)
    busy_key, chosen_key, light_key = jax.random.split(key, 3)
    busy = jax.random.randint(busy_key, (DEVICES,), 0, 2)
    chosen = jax.random.randint(chosen_key, (), 0, DEVICES)
    busy = jnp.where(jnp.arange(DEVICES, dtype=jnp.int32) == chosen, 1, busy)
    light = jax.random.randint(light_key, (LEAVES,), 1, 3)
    per_leaf = jnp.repeat(busy, LEAF_DEV)
    return jnp.where(per_leaf == 1, NEAR, light).astype(jnp.int32)


def draw_cluster_partners(key, part):
    key = jax.random.fold_in(key, 19)
    return distinct_partners(key, DEVICES, N_SUB, COUP)


def draw_cluster_count(key, part):
    key = jax.random.fold_in(key, 23)
    return capped_counts(key, DEVICES, COUP)


def draw_branch_partners(key, part):
    key = jax.random.fold_in(key, 29)
    return distinct_partners(key, N_BRANCH, N_BRANCH, BCOUP)


def draw_branch_count(key, part):
    key = jax.random.fold_in(key, 31)
    return capped_counts(key, N_BRANCH, BCOUP)


def block_levels(rng, shape, shards, low, largest):
    factor_of = 1.0
    for axis_at, parts in shards:
        heights = jax.random.uniform(jax.random.fold_in(jax.random.fold_in(rng, 6), axis_at), (parts,), jnp.float32, low / len(shards), largest / len(shards))
        factor_of = factor_of * jnp.repeat(jnp.exp(heights), shape[axis_at] // parts).reshape((-1,) + (1,) * (len(shape) - 1 - axis_at))
    return factor_of


def bell_draw(rng, extent, spread, limit, cuts=(), held_as=jnp.bfloat16):
    drawn = jax.random.normal(rng, extent, jnp.float32) * spread
    if len(cuts) > 0:
        drawn = block_levels(rng, extent, cuts, -0.22, 0.18) * drawn
    return jnp.clip(drawn, min=-limit, max=limit).astype(held_as)


def setup_inputs(seed: int = 0) -> dict:
    keys = jax.random.split(jax.random.key(seed), 14)
    sources = bell_draw(keys[0], (COLS, NPTS), 1.0, 6.0, ((1, 512),))
    coords = jnp.clip(1.0 * jax.random.uniform(keys[1], (3, NPTS), jnp.float32) ** block_levels(keys[1], (3, NPTS), ((1, 512),), -0.2, 0.2), 0.0, 1.0).astype(jnp.bfloat16)
    leaf_basis = bell_draw(keys[2], (LEAVES, RANK, LEAF), LEAF ** -0.5, 0.375, ((0, 512),))
    leaf_transfer = bell_draw(keys[3], (LEAVES, RANK, RANK), RANK ** -0.5, 0.75, ((0, 512),), jnp.float32)
    cluster_transfer = draw_cluster_transfer(jax.random.fold_in(keys[13], 71), 0)
    near_slots = draw_near_slots(jax.random.fold_in(keys[13], 71), 0)
    near_count = draw_near_count(jax.random.fold_in(keys[13], 71), 0)
    cluster_partners = draw_cluster_partners(jax.random.fold_in(keys[13], 71), 0)
    cluster_count = draw_cluster_count(jax.random.fold_in(keys[13], 71), 0)
    cluster_coupling = bell_draw(keys[9], (DEVICES, COUP, RANK, RANK), (RANK // 4) ** -0.5, 1.5, ((0, 512),), jnp.float32)
    branch_partners = draw_branch_partners(jax.random.fold_in(keys[13], 71), 0)
    branch_count = draw_branch_count(jax.random.fold_in(keys[13], 71), 0)
    branch_coupling_tiles = bell_draw(keys[12], (N_BRANCH, BCOUP, RANK, RANK), (RANK // 4) ** -0.5, 1.5, ((0, 16),), jnp.float32)
    return {"sources": sources, "coords": coords, "leaf_basis": leaf_basis, "leaf_transfer": leaf_transfer, "cluster_transfer": cluster_transfer, "near_slots": near_slots, "near_count": near_count, "cluster_partners": cluster_partners, "cluster_count": cluster_count, "cluster_coupling": cluster_coupling, "branch_partners": branch_partners, "branch_count": branch_count, "branch_coupling_tiles": branch_coupling_tiles}


KERNEL_SCALE = 0.03125
DELTA_SQUARED = 0.01

def kernel_block(source_coords, target_coords):
    sources_f = source_coords.astype(jnp.float32)
    targets_f = target_coords.astype(jnp.float32)
    squared_distance = jnp.zeros((sources_f.shape[1], targets_f.shape[1]), jnp.float32)
    for component in range(3):
        differ = sources_f[component][:, None] - targets_f[component][None, :]
        squared_distance = squared_distance + differ * differ
    return KERNEL_SCALE * lax.rsqrt(squared_distance + DELTA_SQUARED)

def solve_right_transposed(lower, values):
    return lax.linalg.triangular_solve(lower, values, left_side=False, lower=True, transpose_a=True)

def solve_right(lower, values):
    return lax.linalg.triangular_solve(lower, values, left_side=False, lower=True, transpose_a=False)

def reference(sources, coords, leaf_basis, leaf_transfer, cluster_transfer, near_slots, near_count, cluster_partners, cluster_count, cluster_coupling, branch_partners, branch_count, branch_coupling_tiles):
    highest = lax.Precision.HIGHEST
    margin = REACH * LEAF
    padded_source_values = jnp.pad(sources, ((0, 0), (margin, margin)))
    padded_coordinates = jnp.pad(coords, ((0, 0), (margin, margin)))

    def near_leaf(index):
        targets = lax.dynamic_slice_in_dim(coords, index * LEAF, LEAF, 1)
        running = jnp.zeros((COLS, LEAF), jnp.float32)
        for slot in range(NEAR):
            start = (index + near_slots[index, slot]).astype(jnp.int32) * LEAF
            source_coords = lax.dynamic_slice_in_dim(padded_coordinates, start, LEAF, 1)
            source_values = lax.dynamic_slice_in_dim(padded_source_values, start, LEAF, 1)
            block = kernel_block(source_coords, targets).astype(jnp.bfloat16)
            term = jnp.dot(source_values.astype(jnp.float32), block.astype(jnp.float32), preferred_element_type=jnp.float32)
            weight = (slot < near_count[index]).astype(jnp.float32)
            running = running + weight * term
        return running
    near = lax.map(near_leaf, jnp.arange(LEAVES, dtype=jnp.int32))
    near = jnp.transpose(near, (1, 0, 2)).reshape(COLS, NPTS)
    leaf_values = sources.reshape(COLS, LEAVES, LEAF).astype(jnp.float32)
    basis_f = leaf_basis.astype(jnp.float32)
    leaf_up = jnp.einsum('clp,lrp->lcr', leaf_values, basis_f)
    leaf_gram = jnp.einsum('lrp,lsp->lrs', basis_f, basis_f)
    devices_all = N_BRANCH * N_SUB
    leaf_up = leaf_up.reshape(devices_all, LEAF_DEV, COLS, RANK)
    leaf_gram = leaf_gram.reshape(devices_all, LEAF_DEV, RANK, RANK)
    transfers = leaf_transfer.reshape(devices_all, LEAF_DEV, RANK, RANK)
    cluster_up = jnp.einsum('dlcr,dlrs->dcs', leaf_up, transfers, precision=highest)
    half = jnp.einsum('dlrt,dltu->dlru', leaf_gram, transfers, precision=highest)
    cluster_gram = jnp.einsum('dlrs,dlru->dsu', transfers, half, precision=highest)
    cluster_lower = jnp.linalg.cholesky(cluster_gram)
    cluster_ortho = solve_right_transposed(cluster_lower, cluster_up)
    grouped_ortho = cluster_ortho.reshape(N_BRANCH, N_SUB, COLS, RANK)
    grouped_transfer = cluster_transfer.reshape(N_BRANCH, N_SUB, RANK, RANK)
    branch_up = jnp.einsum('bscr,bsrt->bct', grouped_ortho, grouped_transfer, precision=highest)
    branch_gram = jnp.einsum('bsrt,bsru->btu', grouped_transfer, grouped_transfer, precision=highest)
    branch_lower = jnp.linalg.cholesky(branch_gram)
    branch_ortho = solve_right_transposed(branch_lower, branch_up)
    owners = jnp.arange(devices_all, dtype=jnp.int32) // N_SUB * N_SUB
    global_partners = owners[:, None] + cluster_partners
    picked = cluster_ortho[global_partners]
    cluster_live = (jnp.arange(COUP, dtype=jnp.int32)[None, :] < cluster_count[:, None]).astype(jnp.float32)
    cluster_out = jnp.einsum('dkcr,dkrs->dcs', picked * cluster_live[:, :, None, None], cluster_coupling, precision=highest)
    branch_picked = branch_ortho[branch_partners]
    branch_live = (jnp.arange(BCOUP, dtype=jnp.int32)[None, :] < branch_count[:, None]).astype(jnp.float32)
    branch_out = jnp.einsum('bkcr,bkrs->bcs', branch_picked * branch_live[:, :, None, None], branch_coupling_tiles, precision=highest)
    lifted = solve_right(branch_lower, branch_out)
    handed = jnp.einsum('bcr,bsqr->bscq', lifted, grouped_transfer, precision=highest).reshape(devices_all, COLS, RANK)
    down = solve_right(cluster_lower, cluster_out + handed)
    leaf_down = jnp.einsum('dcr,dlqr->dlcq', down, transfers, precision=highest).astype(jnp.bfloat16)
    far = jnp.einsum('dlcq,dlqp->cdlp', leaf_down.astype(jnp.float32), basis_f.reshape(devices_all, LEAF_DEV, RANK, LEAF))
    return near + far.reshape(COLS, NPTS)
```

```python
import functools

import jax
import jax.numpy as jnp
from jax import lax
from jax.experimental import pallas as pl
from jax.experimental.pallas import tpu as pltpu
from jax.sharding import PartitionSpec as P

LEAF = 256
RANK = 64
COLS = 64
HERE = 32
NEAR = 5
COUP = 6
BCOUP = 3
REACH = 2
MARGIN = REACH * LEAF
POINTS = HERE * LEAF
PADDED = POINTS + 2 * MARGIN
FEAT = 16

KERNEL_SCALE = 0.03125
DELTA_SQUARED = 0.01

NX, NY = 4, 8
NZ, NC = 8, 2
N_SUB = NX * NY
N_BRANCH = NZ * NC

HIGHEST = lax.Precision.HIGHEST
MESH = pl.DeviceIdType.MESH
F32 = jnp.float32
BF16 = jnp.bfloat16

CHOL_LEAVES = 16
CHOL_STEPS = RANK // CHOL_LEAVES


def dot_nn(a, b, precision=None):
    return lax.dot_general(
        a, b, (((1,), (0,)), ((), ())), precision=precision, preferred_element_type=F32
    )


def dot_nt(a, b, precision=None):
    return lax.dot_general(
        a, b, (((1,), (1,)), ((), ())), precision=precision, preferred_element_type=F32
    )


def packed(x):
    half = x.shape[0] // 2
    return jnp.concatenate([x[:half], x[half:]], axis=1)


def unpacked(x):
    half = x.shape[1] // 2
    return jnp.concatenate([x[:, :half], x[:, half:]], axis=0)


def diagonal_blocks(x):
    return x[:RANK, :RANK] + x[RANK:, RANK:]


def features(coords):
    c = coords.astype(F32)
    x, y, z = c[0:1], c[1:2], c[2:3]
    norm = x * x + y * y + z * z + 0.5 * DELTA_SQUARED
    n1 = norm.astype(BF16).astype(F32)
    n2 = (norm - n1).astype(BF16).astype(F32)
    n3 = norm - n1 - n2
    row = lax.broadcasted_iota(jnp.int32, (FEAT, coords.shape[1]), 0)
    ones = jnp.ones_like(norm)

    def stacked(parts):
        out = jnp.zeros((FEAT, coords.shape[1]), F32)
        for at, part in enumerate(parts):
            out = jnp.where(row == at, part, out)
        return out.astype(BF16)

    source = stacked([x, y, z, n1, n2, n3, ones, ones, ones])
    target = stacked([-2.0 * x, -2.0 * y, -2.0 * z, ones, ones, ones, n1, n2, n3])
    return source, target


def eliminate(k, left, right):
    for ref in (left, right):
        square = ref[:, 0:128]
        lane = lax.broadcasted_iota(jnp.int32, square.shape, 1)
        row = lax.broadcasted_iota(jnp.int32, (RANK, 1), 0)
        column = jnp.sum(jnp.where(lane == k, square, 0.0), axis=1, keepdims=True)
        pivot_row = ref[pl.ds(k, 1), :]
        lane_row = lax.broadcasted_iota(jnp.int32, pivot_row.shape, 1)
        pivot = jnp.sum(jnp.where(lane_row == k, pivot_row, 0.0), axis=1, keepdims=True)
        factor = jnp.where(row > k, column * (1.0 / pivot), 0.0)
        ref[...] = ref[...] - factor * pivot_row


def row_scale(square):
    row = lax.broadcasted_iota(jnp.int32, (RANK, 128), 0)
    lane = lax.broadcasted_iota(jnp.int32, (RANK, 128), 1)
    pivots = jnp.sum(jnp.where(row == lane, square, 0.0), axis=1, keepdims=True)
    return lax.rsqrt(pivots)


def main_kernel(
    sources,
    coords,
    basis_hbm,
    transfer_hbm,
    cluster_transfer,
    near_slots,
    near_count,
    cluster_partners,
    cluster_count,
    coupling,
    branch_partners,
    branch_count,
    branch_tiles,
    near_out,
    vt_out,
    down_out,
    basis,
    transfer,
    window,
    source_feat,
    target_feat,
    source_feat_t,
    all_transfer,
    all_transfer_t,
    all_ortho,
    all_branch,
    left,
    right,
    local_sems,
    halo_send,
    halo_recv,
    send_sems,
    recv_sems,
):
    branch = lax.axis_index("branch")
    sub = lax.axis_index("sub")
    sx, sy = sub % NX, sub // NX
    bz, bc = branch // NC, branch % NC

    load_basis = pltpu.make_async_copy(basis_hbm, basis, local_sems.at[0])
    load_transfer = pltpu.make_async_copy(transfer_hbm, transfer, local_sems.at[1])
    load_sources = pltpu.make_async_copy(
        sources, window.at[:, pl.ds(MARGIN, POINTS)], local_sems.at[2]
    )
    load_basis.start()
    load_transfer.start()
    load_sources.start()

    def sub_peer(o):
        return ((sy + o // NX) % NY) * NX + (sx + o % NX) % NX

    def branch_peer(o):
        return ((bz + o // NC) % NZ) * NC + (bc + o % NC) % NC

    here = branch * N_SUB + sub
    total = N_BRANCH * N_SUB
    after = (here + 1) % total
    before = (here + total - 1) % total
    after_id = (after // N_SUB, after % N_SUB)
    before_id = (before // N_SUB, before % N_SUB)

    barrier = pltpu.get_barrier_semaphore()

    @pl.loop(1, N_SUB)
    def _(o):
        pl.semaphore_signal(
            barrier, inc=1, device_id=(branch, sub_peer(o)), device_id_type=MESH
        )

    @pl.loop(1, N_BRANCH)
    def _(o):
        pl.semaphore_signal(
            barrier, inc=1, device_id=(branch_peer(o), sub), device_id_type=MESH
        )

    pl.semaphore_signal(barrier, inc=1, device_id=after_id, device_id_type=MESH)
    pl.semaphore_signal(barrier, inc=1, device_id=before_id, device_id_type=MESH)

    own_transfer = cluster_transfer[0]
    all_transfer[0] = packed(own_transfer).astype(BF16)
    feat_source, feat_target = features(coords[...])
    source_feat[:, MARGIN : MARGIN + POINTS] = feat_source
    target_feat[...] = feat_target

    pl.semaphore_wait(barrier, N_SUB - 1 + N_BRANCH - 1 + 2)

    def sub_copy(buffer, slot, o):
        return pltpu.make_async_remote_copy(
            src_ref=buffer.at[0],
            dst_ref=buffer.at[o],
            send_sem=send_sems.at[slot],
            recv_sem=recv_sems.at[slot],
            device_id=(branch, sub_peer(o)),
            device_id_type=MESH,
        )

    def all_copies(buffer, slot, count):
        return pltpu.make_async_remote_copy(
            src_ref=buffer.at[pl.ds(1, count - 1)],
            dst_ref=buffer.at[pl.ds(1, count - 1)],
            send_sem=send_sems.at[slot],
            recv_sem=recv_sems.at[slot],
            device_id=(branch, sub_peer(1)),
            device_id_type=MESH,
        )

    @pl.loop(1, N_SUB)
    def _(o):
        sub_copy(all_transfer, 0, o).start()

    def halo_copy(src, dst, at, device):
        return pltpu.make_async_remote_copy(
            src_ref=src,
            dst_ref=dst,
            send_sem=halo_send.at[at],
            recv_sem=halo_recv.at[at],
            device_id=device,
            device_id_type=MESH,
        )

    low, high = pl.ds(0, MARGIN), pl.ds(MARGIN + POINTS, MARGIN)
    halos = [
        halo_copy(
            sources.at[:, pl.ds(POINTS - MARGIN, MARGIN)], window.at[:, low], 0, after_id
        ),
        halo_copy(sources.at[:, pl.ds(0, MARGIN)], window.at[:, high], 1, before_id),
        halo_copy(
            source_feat.at[:, pl.ds(POINTS, MARGIN)], source_feat.at[:, low], 2, after_id
        ),
        halo_copy(
            source_feat.at[:, pl.ds(MARGIN, MARGIN)], source_feat.at[:, high], 3, before_id
        ),
    ]
    for copy in halos:
        copy.start()

    def transpose_features(at):
        columns = pl.ds(pl.multiple_of(at * LEAF, LEAF), LEAF)
        block = source_feat[:, columns].astype(F32)
        source_feat_t[columns, :] = block.T.astype(BF16)

    @pl.loop(REACH, REACH + HERE)
    def _(at):
        transpose_features(at)

    load_basis.wait()
    load_transfer.wait()
    load_sources.wait()

    def climb(at, total_up):
        columns = pl.ds(pl.multiple_of(at * LEAF, LEAF), LEAF)
        block = transfer[at].T
        block_high = block.astype(BF16)
        block_low = (block - block_high.astype(F32)).astype(BF16)
        leaf_basis = basis[at]
        vt = (dot_nn(block_high, leaf_basis) + dot_nn(block_low, leaf_basis)).astype(BF16)
        vt_out[:, columns] = vt
        values = window[:, pl.ds(pl.multiple_of(MARGIN + at * LEAF, LEAF), LEAF)]
        return total_up + dot_nt(vt, jnp.concatenate([vt, values], axis=0))

    gram_up = lax.fori_loop(0, HERE, climb, jnp.zeros((RANK, 2 * RANK), F32), unroll=4)
    row = lax.broadcasted_iota(jnp.int32, (RANK, 128), 0)
    lane = lax.broadcasted_iota(jnp.int32, (RANK, 128), 1)
    left[:, 0:128] = gram_up
    left[:, 128:256] = jnp.where(row == lane, 1.0, 0.0)

    all_copies(all_transfer, 0, N_SUB).wait_recv()
    stack = all_transfer[...].reshape(N_SUB * RANK // 2, 2 * RANK)
    stack_t = stack.astype(F32).T.astype(BF16)
    all_transfer_t[...] = stack_t
    branch_gram = diagonal_blocks(dot_nn(stack_t, stack))
    right[...] = jnp.concatenate(
        [branch_gram, jnp.where(row == lane, 1.0, 0.0)[:, :RANK]], axis=1
    )

    def near_leaf(at):
        target = target_feat[:, pl.ds(pl.multiple_of(at * LEAF, LEAF), LEAF)]
        live = near_count[at]
        result = jnp.zeros((COLS, LEAF), F32)
        for shift in range(NEAR):
            weight = jnp.int32(0)
            for slot in range(NEAR):
                weight = weight + jnp.where(
                    jnp.logical_and(near_slots[at, slot] == shift, slot < live), 1, 0
                )
            points = pl.ds(pl.multiple_of((at + shift) * LEAF, LEAF), LEAF)
            distance = dot_nn(source_feat_t[points, :], target)
            block = lax.rsqrt(distance).astype(BF16)
            values = window[:, points]
            values = values * jnp.full(values.shape, weight.astype(F32)).astype(BF16)
            result = result + dot_nn(values, block)
        near_out[:, pl.ds(pl.multiple_of(at * LEAF, LEAF), LEAF)] = result * KERNEL_SCALE

    @pl.loop(0, CHOL_LEAVES)
    def _(it):
        near_leaf(it + REACH)
        for j in range(CHOL_STEPS):
            eliminate(it * CHOL_STEPS + j, left, right)

    scale = row_scale(left[:, 0:128])
    ortho_t = left[:, RANK : 2 * RANK] * scale
    all_ortho[0] = packed(ortho_t).astype(BF16)

    @pl.loop(1, N_SUB)
    def _(o):
        sub_copy(all_ortho, 1, o).start()

    inverse = left[:, 128 : 128 + RANK] * scale
    inverse_t = inverse.T
    branch_inverse = right[:, RANK:] * row_scale(right[...])
    cluster_map = dot_nt(inverse_t, coupling[0].reshape(COUP * RANK, RANK), HIGHEST)
    handed = dot_nt(dot_nn(inverse_t, own_transfer, HIGHEST), branch_inverse, HIGHEST)
    branch_map = dot_nt(handed, branch_tiles[0].reshape(BCOUP * RANK, RANK), HIGHEST)

    @pl.loop(REACH + CHOL_LEAVES, HERE - REACH)
    def _(at):
        near_leaf(at)

    all_copies(all_ortho, 1, N_SUB).wait_recv()
    branch_up_t = diagonal_blocks(
        dot_nn(all_transfer_t[...], all_ortho[...].reshape(N_SUB * RANK // 2, 2 * RANK))
    )
    branch_ortho_t = dot_nn(branch_inverse, branch_up_t, HIGHEST)
    all_branch[0] = packed(branch_ortho_t).astype(BF16)

    @pl.loop(1, N_BRANCH)
    def _(o):
        pltpu.make_async_remote_copy(
            src_ref=all_branch.at[0],
            dst_ref=all_branch.at[o],
            send_sem=send_sems.at[2],
            recv_sem=recv_sems.at[2],
            device_id=(branch_peer(o), sub),
            device_id_type=MESH,
        ).start()

    picked = []
    for k in range(COUP):
        partner = cluster_partners[0, k]
        slot = ((sy - partner // NX + NY) % NY) * NX + (sx - partner % NX + NX) % NX
        alive = jnp.where(k < cluster_count[0], 1.0, 0.0)
        picked.append(unpacked(all_ortho[slot].astype(F32)) * alive)
    down_t = dot_nn(cluster_map, jnp.concatenate(picked, axis=0), HIGHEST)

    for copy in halos:
        copy.wait_recv()
    keep_low = jnp.where(here == 0, 0.0, 1.0)
    keep_high = jnp.where(here == total - 1, 0.0, 1.0)
    for columns, keep in ((slice(0, MARGIN), keep_low), (slice(MARGIN + POINTS, PADDED), keep_high)):
        edge = window[:, columns]
        window[:, columns] = edge * jnp.full(edge.shape, keep).astype(BF16)
    for at in (0, 1, HERE + REACH, HERE + REACH + 1):
        transpose_features(at)

    @pl.loop(0, 2 * REACH)
    def _(it):
        near_leaf(jnp.where(it < REACH, it, HERE - 2 * REACH + it))

    all_copies(all_branch, 2, N_BRANCH).wait_recv()
    picked = []
    for k in range(BCOUP):
        partner = branch_partners[0, k]
        slot = ((bz - partner // NC + NZ) % NZ) * NC + (bc - partner % NC + NC) % NC
        alive = jnp.where(k < branch_count[0], 1.0, 0.0)
        picked.append(unpacked(all_branch[slot].astype(F32)) * alive)
    down_t = down_t + dot_nn(branch_map, jnp.concatenate(picked, axis=0), HIGHEST)
    down_out[...] = down_t.T

    for copy in halos:
        copy.wait_send()
    all_copies(all_transfer, 0, N_SUB).wait_send()
    all_copies(all_ortho, 1, N_SUB).wait_send()
    all_copies(all_branch, 2, N_BRANCH).wait_send()


def far_kernel(near, vt, down, out):
    high = down[...].astype(BF16)
    low = (down[...] - high.astype(F32)).astype(BF16)
    out[...] = near[...] + dot_nn(high, vt[...]) + dot_nn(low, vt[...])


def shards(
    sources,
    coords,
    leaf_basis,
    leaf_transfer,
    cluster_transfer,
    near_slots,
    near_count,
    cluster_partners,
    cluster_count,
    cluster_coupling,
    branch_partners,
    branch_count,
    branch_coupling_tiles,
):
    vmem = pl.BlockSpec(memory_space=pltpu.VMEM)
    smem = pl.BlockSpec(memory_space=pltpu.SMEM)
    hbm = pl.BlockSpec(memory_space=pl.ANY)
    near, vt, down = pl.pallas_call(
        main_kernel,
        out_shape=(
            jax.ShapeDtypeStruct((COLS, POINTS), F32),
            jax.ShapeDtypeStruct((RANK, POINTS), BF16),
            jax.ShapeDtypeStruct((COLS, RANK), F32),
        ),
        in_specs=[
            hbm,
            vmem,
            hbm,
            hbm,
            vmem,
            smem,
            smem,
            smem,
            smem,
            vmem,
            smem,
            smem,
            vmem,
        ],
        out_specs=(vmem, vmem, vmem),
        scratch_shapes=[
            pltpu.VMEM((HERE, RANK, LEAF), BF16),
            pltpu.VMEM((HERE, RANK, RANK), F32),
            pltpu.VMEM((COLS, PADDED), BF16),
            pltpu.VMEM((FEAT, PADDED), BF16),
            pltpu.VMEM((FEAT, POINTS), BF16),
            pltpu.VMEM((PADDED, FEAT), BF16),
            pltpu.VMEM((N_SUB, RANK // 2, 2 * RANK), BF16),
            pltpu.VMEM((2 * RANK, N_SUB * RANK // 2), BF16),
            pltpu.VMEM((N_SUB, RANK // 2, 2 * RANK), BF16),
            pltpu.VMEM((N_BRANCH, RANK // 2, 2 * RANK), BF16),
            pltpu.VMEM((RANK, 256), F32),
            pltpu.VMEM((RANK, 128), F32),
            pltpu.SemaphoreType.DMA((3,)),
            pltpu.SemaphoreType.DMA((4,)),
            pltpu.SemaphoreType.DMA((4,)),
            pltpu.SemaphoreType.DMA((3,)),
            pltpu.SemaphoreType.DMA((3,)),
        ],
        compiler_params=pltpu.CompilerParams(
            collective_id=0, has_side_effects=True, vmem_limit_bytes=40 * 2**20
        ),
        name="h2_main",
    )(
        sources,
        coords,
        leaf_basis,
        leaf_transfer,
        cluster_transfer,
        near_slots,
        near_count,
        cluster_partners,
        cluster_count,
        cluster_coupling,
        branch_partners,
        branch_count,
        branch_coupling_tiles,
    )
    chunk = 2048
    return pl.pallas_call(
        far_kernel,
        out_shape=jax.ShapeDtypeStruct((COLS, POINTS), F32),
        grid=(POINTS // chunk,),
        in_specs=[
            pl.BlockSpec((COLS, chunk), lambda i: (0, i)),
            pl.BlockSpec((RANK, chunk), lambda i: (0, i)),
            pl.BlockSpec((COLS, RANK), lambda i: (0, 0)),
        ],
        out_specs=pl.BlockSpec((COLS, chunk), lambda i: (0, i)),
        compiler_params=pltpu.CompilerParams(vmem_limit_bytes=32 * 2**20),
        name="h2_far",
    )(near, vt, down)


def solution(mesh):
    return jax.shard_map(
        shards,
        mesh=mesh,
        in_specs=(
            P(None, ("branch", "sub")),
            P(None, ("branch", "sub")),
            P(("branch", "sub"), None, None),
            P(("branch", "sub"), None, None),
            P(("branch", "sub"), None, None),
            P(("branch", "sub"), None),
            P(("branch", "sub")),
            P(("branch", "sub"), None),
            P(("branch", "sub")),
            P(("branch", "sub"), None, None, None),
            P("branch", None),
            P("branch"),
            P("branch", None, None, None),
        ),
        out_specs=P(None, ("branch", "sub")),
        check_vma=False,
    )
```

```python
import functools

import jax
import jax.numpy as jnp
from jax import lax
from jax.experimental import pallas as pl
from jax.experimental.pallas import tpu as pltpu
from jax.sharding import PartitionSpec as P

LEAF = 256
RANK = 64
COLS = 64
HERE = 32
NEAR = 5
COUP = 6
BCOUP = 3
REACH = 2
MARGIN = REACH * LEAF
POINTS = HERE * LEAF
PADDED = POINTS + 2 * MARGIN
FEAT = 16

KERNEL_SCALE = 0.03125
DELTA_SQUARED = 0.01

NX, NY = 4, 8
NZ, NC = 8, 2
N_SUB = NX * NY
N_BRANCH = NZ * NC

HIGHEST = lax.Precision.HIGHEST
MESH = pl.DeviceIdType.MESH
F32 = jnp.float32
BF16 = jnp.bfloat16

FIRST_PAIRS = 8


def dot_nn(a, b, precision=None):
    return lax.dot_general(
        a, b, (((1,), (0,)), ((), ())), precision=precision, preferred_element_type=F32
    )


def dot_nt(a, b, precision=None):
    return lax.dot_general(
        a, b, (((1,), (1,)), ((), ())), precision=precision, preferred_element_type=F32
    )


def packed(x):
    half = x.shape[0] // 2
    return jnp.concatenate([x[:half], x[half:]], axis=1)


def unpacked(x):
    half = x.shape[1] // 2
    return jnp.concatenate([x[:, :half], x[:, half:]], axis=0)


def diagonal_blocks(x):
    return x[:RANK, :RANK] + x[RANK:, RANK:]


def features(coords):
    c = coords.astype(F32)
    x, y, z = c[0:1], c[1:2], c[2:3]
    norm = x * x + y * y + z * z + 0.5 * DELTA_SQUARED
    n1 = norm.astype(BF16).astype(F32)
    n2 = (norm - n1).astype(BF16).astype(F32)
    n3 = norm - n1 - n2
    row = lax.broadcasted_iota(jnp.int32, (FEAT, coords.shape[1]), 0)
    ones = jnp.ones_like(norm)

    def stacked(parts):
        out = jnp.zeros((FEAT, coords.shape[1]), F32)
        for at, part in enumerate(parts):
            out = jnp.where(row == at, part, out)
        return out.astype(BF16)

    source = stacked([x, y, z, n1, n2, n3, ones, ones, ones])
    target = stacked([-2.0 * x, -2.0 * y, -2.0 * z, ones, ones, ones, n1, n2, n3])
    return source, target


def leaf_columns(at):
    return pl.ds(pl.multiple_of(at * LEAF, LEAF), LEAF)


def prepare_features(at, coords, source_feat, source_feat_t, target_feat):
    feat_source, feat_target = features(coords[:, leaf_columns(at)])
    source_feat[:, leaf_columns(at + REACH)] = feat_source
    source_feat_t[leaf_columns(at + REACH), :] = feat_source.astype(F32).T.astype(BF16)
    target_feat[:, leaf_columns(at)] = feat_target


def transpose_features(at, source_feat, source_feat_t):
    block = source_feat[:, leaf_columns(at)].astype(F32)
    source_feat_t[leaf_columns(at), :] = block.T.astype(BF16)


def eliminate(k, ref):
    square = ref[:, 0:128]
    lane = lax.broadcasted_iota(jnp.int32, square.shape, 1)
    row = lax.broadcasted_iota(jnp.int32, (RANK, 1), 0)
    column = jnp.sum(jnp.where(lane == k, square, 0.0), axis=1, keepdims=True)
    pivot_row = ref[pl.ds(k, 1), :]
    lane_row = lax.broadcasted_iota(jnp.int32, pivot_row.shape, 1)
    pivot = jnp.sum(jnp.where(lane_row == k, pivot_row, 0.0), axis=1, keepdims=True)
    factor = jnp.where(row > k, column * (1.0 / pivot), 0.0)
    ref[...] = ref[...] - factor * pivot_row


def row_scale(square):
    row = lax.broadcasted_iota(jnp.int32, (RANK, 128), 0)
    lane = lax.broadcasted_iota(jnp.int32, (RANK, 128), 1)
    pivots = jnp.sum(jnp.where(row == lane, square, 0.0), axis=1, keepdims=True)
    return lax.rsqrt(pivots)


def climb_leaves(low, high, total, transfer, basis, window, vt_out):
    def climb(at, total):
        columns = pl.ds(pl.multiple_of(at * LEAF, LEAF), LEAF)
        block = transfer[at].T
        block_high = block.astype(BF16)
        block_low = (block - block_high.astype(F32)).astype(BF16)
        leaf_basis = basis[at]
        vt = (dot_nn(block_high, leaf_basis) + dot_nn(block_low, leaf_basis)).astype(BF16)
        vt_out[:, columns] = vt
        values = window[:, pl.ds(pl.multiple_of(MARGIN + at * LEAF, LEAF), LEAF)]
        return total + dot_nt(vt, jnp.concatenate([vt, values], axis=0))

    return lax.fori_loop(low, high, climb, total, unroll=4)


def near_start(at, made, source_feat_t, target_feat):
    target = target_feat[:, leaf_columns(at)]
    for shift in range(NEAR):
        distance = dot_nn(source_feat_t[leaf_columns(at + shift), :], target)
        made[shift * LEAF : (shift + 1) * LEAF, :] = lax.rsqrt(distance).astype(BF16)


def near_step(at, following, used, made, near_slots, near_count, source_feat_t, target_feat, window, near_out):
    target = target_feat[:, leaf_columns(following)]
    live = near_count[at]
    result = jnp.zeros((COLS, LEAF), F32)
    for shift in range(NEAR):
        weight = jnp.int32(0)
        for slot in range(NEAR):
            weight = weight + jnp.where(
                jnp.logical_and(near_slots[slot, at] == shift, slot < live), 1, 0
            )
        values = window[:, leaf_columns(at + shift)]
        values = values * jnp.full(values.shape, weight.astype(F32)).astype(BF16)
        rows = slice(shift * LEAF, (shift + 1) * LEAF)
        result = result + dot_nn(values, used[rows, :])
        distance = dot_nn(source_feat_t[leaf_columns(following + shift), :], target)
        made[rows, :] = lax.rsqrt(distance).astype(BF16)
    near_out[:, leaf_columns(at)] = result * KERNEL_SCALE


def main_kernel(
    cluster_count,
    branch_count,
    sources,
    coords_hbm,
    basis_hbm,
    transfer_hbm,
    cluster_transfer_hbm,
    near_slots_hbm,
    near_count_hbm,
    cluster_partners_hbm,
    coupling_hbm,
    branch_partners_hbm,
    branch_tiles_hbm,
    near_out,
    vt_out,
    down_out,
    coords,
    basis,
    transfer,
    cluster_transfer,
    near_slots,
    near_count,
    cluster_partners,
    coupling,
    branch_partners,
    branch_tiles,
    window,
    source_feat,
    target_feat,
    source_feat_t,
    all_transfer,
    all_transfer_t,
    all_ortho,
    all_branch,
    left,
    right,
    blocks_even,
    blocks_odd,
    local_sems,
    halo_send,
    halo_recv,
    send_sems,
    recv_sems,
):
    branch = lax.axis_index("branch")
    sub = lax.axis_index("sub")
    sx, sy = sub % NX, sub // NX
    bz, bc = branch // NC, branch % NC

    loads = [
        pltpu.make_async_copy(src, dst, local_sems.at[at])
        for at, (src, dst) in enumerate(
            (
                (transfer_hbm, transfer),
                (basis_hbm, basis),
                (sources, window.at[:, pl.ds(MARGIN, POINTS)]),
                (cluster_transfer_hbm, cluster_transfer),
                (coords_hbm, coords),
                (near_slots_hbm, near_slots),
                (near_count_hbm, near_count),
                (cluster_partners_hbm, cluster_partners),
                (coupling_hbm, coupling),
                (branch_partners_hbm, branch_partners),
                (branch_tiles_hbm, branch_tiles),
            )
        )
    ]
    for load in loads:
        load.start()

    at_x = [(sx + d) % NX for d in range(NX)]
    at_y = [(sy + d) % NY * NX for d in range(NY)]
    at_z = [(bz + d) % NZ * NC for d in range(NZ)]
    at_c = [(bc + d) % NC for d in range(NC)]
    sub_peers = [at_y[o // NX] + at_x[o % NX] for o in range(N_SUB)]
    branch_peers = [at_z[o // NC] + at_c[o % NC] for o in range(N_BRANCH)]

    here = branch * N_SUB + sub
    total = N_BRANCH * N_SUB
    after = (here + 1) % total
    before = (here + total - 1) % total
    after_id = (after // N_SUB, after % N_SUB)
    before_id = (before // N_SUB, before % N_SUB)

    barrier = pltpu.get_barrier_semaphore()
    for device in (
        [(branch, peer) for peer in sub_peers[1:]]
        + [(peer, sub) for peer in branch_peers[1:]]
        + [after_id, before_id]
    ):
        pl.semaphore_signal(barrier, inc=1, device_id=device, device_id_type=MESH)

    def gather_copy(src, dst, slot, device):
        return pltpu.make_async_remote_copy(
            src_ref=src,
            dst_ref=dst,
            send_sem=send_sems.at[slot],
            recv_sem=recv_sems.at[slot],
            device_id=device,
            device_id_type=MESH,
        )

    def all_copies(buffer, slot, count):
        others = buffer.at[pl.ds(1, count - 1)]
        return gather_copy(others, others, slot, (branch, sub_peers[1]))

    def start_sub(buffer, slot):
        for o in range(1, N_SUB):
            gather_copy(buffer.at[0], buffer.at[o], slot, (branch, sub_peers[o])).start()

    def halo_copy(src, dst, at, device):
        return pltpu.make_async_remote_copy(
            src_ref=src,
            dst_ref=dst,
            send_sem=halo_send.at[at],
            recv_sem=halo_recv.at[at],
            device_id=device,
            device_id_type=MESH,
        )

    low, high = pl.ds(0, MARGIN), pl.ds(MARGIN + POINTS, MARGIN)
    halos = [
        halo_copy(
            sources.at[:, pl.ds(POINTS - MARGIN, MARGIN)], window.at[:, low], 0, after_id
        ),
        halo_copy(sources.at[:, pl.ds(0, MARGIN)], window.at[:, high], 1, before_id),
        halo_copy(
            source_feat.at[:, pl.ds(POINTS, MARGIN)], source_feat.at[:, low], 2, after_id
        ),
        halo_copy(
            source_feat.at[:, pl.ds(MARGIN, MARGIN)], source_feat.at[:, high], 3, before_id
        ),
    ]

    for load in loads[:4]:
        load.wait()
    own_transfer = cluster_transfer[0]
    all_transfer[0] = packed(own_transfer).astype(BF16)

    climb = functools.partial(
        climb_leaves, transfer=transfer, basis=basis, window=window, vt_out=vt_out
    )
    gram_up = climb(0, HERE // 2, jnp.zeros((RANK, 2 * RANK), F32))
    pl.semaphore_wait(barrier, N_SUB - 1 + N_BRANCH - 1 + 2)
    start_sub(all_transfer, 0)
    halos[0].start()
    halos[1].start()
    gram_up = climb(HERE // 2, HERE, gram_up)

    row = lax.broadcasted_iota(jnp.int32, (RANK, 128), 0)
    lane = lax.broadcasted_iota(jnp.int32, (RANK, 128), 1)
    identity = jnp.where(row == lane, 1.0, 0.0)
    left[:, 0:128] = gram_up
    left[:, 128:256] = identity
    for load in loads[4:]:
        load.wait()

    @pl.loop(0, HERE)
    def _(it):
        prepare_features(it, coords, source_feat, source_feat_t, target_feat)
        for j in range(RANK // HERE):
            eliminate(it * (RANK // HERE) + j, left)

    scale = row_scale(left[:, 0:128])
    ortho_t = left[:, RANK : 2 * RANK] * scale
    all_ortho[0] = packed(ortho_t).astype(BF16)
    start_sub(all_ortho, 1)
    halos[2].start()
    halos[3].start()

    near_of = dict(
        near_slots=near_slots,
        near_count=near_count,
        source_feat_t=source_feat_t,
        target_feat=target_feat,
        window=window,
        near_out=near_out,
    )
    near_start(REACH, blocks_even, source_feat_t, target_feat)

    def near_pair(at, following):
        near_step(at, at + 1, blocks_even, blocks_odd, **near_of)
        near_step(at + 1, following, blocks_odd, blocks_even, **near_of)

    all_copies(all_transfer, 0, N_SUB).wait_recv()
    stack = all_transfer[...].reshape(N_SUB * RANK // 2, 2 * RANK)
    stack_t = stack.astype(F32).T.astype(BF16)
    all_transfer_t[...] = stack_t
    branch_gram = diagonal_blocks(dot_nn(stack_t, stack))
    right[...] = jnp.concatenate([branch_gram, identity[:, :RANK]], axis=1)

    @pl.loop(0, FIRST_PAIRS)
    def _(it):
        near_pair(REACH + 2 * it, REACH + 2 * it + 2)
        for j in range(RANK // FIRST_PAIRS):
            eliminate(it * (RANK // FIRST_PAIRS) + j, right)

    inverse = left[:, 128 : 128 + RANK] * scale
    inverse_t = inverse.T
    branch_inverse = right[:, RANK:] * row_scale(right[...])

    all_copies(all_ortho, 1, N_SUB).wait_recv()
    branch_up_t = diagonal_blocks(
        dot_nn(all_transfer_t[...], all_ortho[...].reshape(N_SUB * RANK // 2, 2 * RANK))
    )
    branch_ortho_t = dot_nn(branch_inverse, branch_up_t, HIGHEST)
    all_branch[0] = packed(branch_ortho_t).astype(BF16)
    for o in range(1, N_BRANCH):
        gather_copy(all_branch.at[0], all_branch.at[o], 2, (branch_peers[o], sub)).start()

    cluster_map = dot_nt(inverse_t, coupling[0].reshape(COUP * RANK, RANK), HIGHEST)
    handed = dot_nt(dot_nn(inverse_t, own_transfer, HIGHEST), branch_inverse, HIGHEST)
    branch_map = dot_nt(handed, branch_tiles[0].reshape(BCOUP * RANK, RANK), HIGHEST)
    picked = []
    for k in range(COUP):
        partner = cluster_partners[0, k]
        slot = ((sy - partner // NX + NY) % NY) * NX + (sx - partner % NX + NX) % NX
        alive = jnp.where(k < cluster_count[0], 1.0, 0.0)
        picked.append(unpacked(all_ortho[slot].astype(F32)) * alive)
    down_t = dot_nn(cluster_map, jnp.concatenate(picked, axis=0), HIGHEST)

    @pl.loop(FIRST_PAIRS, (HERE - 2 * REACH) // 2)
    def _(it):
        near_pair(
            REACH + 2 * it, jnp.minimum(REACH + 2 * it + 2, HERE - REACH - 1)
        )

    for copy in halos:
        copy.wait_recv()
    keep_low = jnp.where(here == 0, 0.0, 1.0)
    keep_high = jnp.where(here == total - 1, 0.0, 1.0)
    for columns, keep in ((slice(0, MARGIN), keep_low), (slice(MARGIN + POINTS, PADDED), keep_high)):
        edge = window[:, columns]
        window[:, columns] = edge * jnp.full(edge.shape, keep).astype(BF16)
    for at in (0, 1, HERE + REACH, HERE + REACH + 1):
        transpose_features(at, source_feat, source_feat_t)
    near_start(0, blocks_even, source_feat_t, target_feat)
    near_pair(0, HERE - REACH)
    near_pair(HERE - REACH, HERE - 1)

    all_copies(all_branch, 2, N_BRANCH).wait_recv()
    picked = []
    for k in range(BCOUP):
        partner = branch_partners[0, k]
        slot = ((bz - partner // NC + NZ) % NZ) * NC + (bc - partner % NC + NC) % NC
        alive = jnp.where(k < branch_count[0], 1.0, 0.0)
        picked.append(unpacked(all_branch[slot].astype(F32)) * alive)
    down_t = down_t + dot_nn(branch_map, jnp.concatenate(picked, axis=0), HIGHEST)
    down_out[...] = down_t.T

    for copy in halos:
        copy.wait_send()
    all_copies(all_transfer, 0, N_SUB).wait_send()
    all_copies(all_ortho, 1, N_SUB).wait_send()
    all_copies(all_branch, 2, N_BRANCH).wait_send()


def far_kernel(near, vt, down, out):
    high = down[...].astype(BF16)
    low = (down[...] - high.astype(F32)).astype(BF16)
    out[...] = near[...] + dot_nn(high, vt[...]) + dot_nn(low, vt[...])


def shards(
    sources,
    coords,
    leaf_basis,
    leaf_transfer,
    cluster_transfer,
    near_slots,
    near_count,
    cluster_partners,
    cluster_count,
    cluster_coupling,
    branch_partners,
    branch_count,
    branch_coupling_tiles,
):
    vmem = pl.BlockSpec(memory_space=pltpu.VMEM)
    smem = pl.BlockSpec(memory_space=pltpu.SMEM)
    hbm = pl.BlockSpec(memory_space=pltpu.HBM)
    near, vt, down = pl.pallas_call(
        main_kernel,
        out_shape=(
            jax.ShapeDtypeStruct((COLS, POINTS), F32),
            jax.ShapeDtypeStruct((RANK, POINTS), BF16),
            jax.ShapeDtypeStruct((COLS, RANK), F32),
        ),
        in_specs=[smem] * 2 + [hbm] * 11,
        out_specs=(vmem, vmem, vmem),
        scratch_shapes=[
            pltpu.VMEM((3, POINTS), BF16),
            pltpu.VMEM((HERE, RANK, LEAF), BF16),
            pltpu.VMEM((HERE, RANK, RANK), F32),
            pltpu.VMEM((1, RANK, RANK), F32),
            pltpu.SMEM((NEAR, HERE), jnp.int32),
            pltpu.SMEM((HERE,), jnp.int32),
            pltpu.SMEM((1, COUP), jnp.int32),
            pltpu.VMEM((1, COUP, RANK, RANK), F32),
            pltpu.SMEM((1, BCOUP), jnp.int32),
            pltpu.VMEM((1, BCOUP, RANK, RANK), F32),
            pltpu.VMEM((COLS, PADDED), BF16),
            pltpu.VMEM((FEAT, PADDED), BF16),
            pltpu.VMEM((FEAT, POINTS), BF16),
            pltpu.VMEM((PADDED, FEAT), BF16),
            pltpu.VMEM((N_SUB, RANK // 2, 2 * RANK), BF16),
            pltpu.VMEM((2 * RANK, N_SUB * RANK // 2), BF16),
            pltpu.VMEM((N_SUB, RANK // 2, 2 * RANK), BF16),
            pltpu.VMEM((N_BRANCH, RANK // 2, 2 * RANK), BF16),
            pltpu.VMEM((RANK, 256), F32),
            pltpu.VMEM((RANK, 128), F32),
            pltpu.VMEM((NEAR * LEAF, LEAF), BF16),
            pltpu.VMEM((NEAR * LEAF, LEAF), BF16),
            pltpu.SemaphoreType.DMA((11,)),
            pltpu.SemaphoreType.DMA((4,)),
            pltpu.SemaphoreType.DMA((4,)),
            pltpu.SemaphoreType.DMA((3,)),
            pltpu.SemaphoreType.DMA((3,)),
        ],
        compiler_params=pltpu.CompilerParams(
            collective_id=0, has_side_effects=True, vmem_limit_bytes=40 * 2**20
        ),
        name="h2_main",
    )(
        cluster_count,
        branch_count,
        *(
            pltpu.with_memory_space_constraint(operand, pltpu.HBM)
            for operand in (
                sources,
                coords,
                leaf_basis,
                leaf_transfer,
                cluster_transfer,
                near_slots.T,
                near_count,
                cluster_partners,
                cluster_coupling,
                branch_partners,
                branch_coupling_tiles,
            )
        )
    )
    chunk = 2048
    return pl.pallas_call(
        far_kernel,
        out_shape=jax.ShapeDtypeStruct((COLS, POINTS), F32),
        grid=(POINTS // chunk,),
        in_specs=[
            pl.BlockSpec((COLS, chunk), lambda i: (0, i)),
            pl.BlockSpec((RANK, chunk), lambda i: (0, i)),
            pl.BlockSpec((COLS, RANK), lambda i: (0, 0)),
        ],
        out_specs=pl.BlockSpec((COLS, chunk), lambda i: (0, i)),
        compiler_params=pltpu.CompilerParams(vmem_limit_bytes=32 * 2**20),
        name="h2_far",
    )(near, vt, down)


def solution(mesh):
    return jax.shard_map(
        shards,
        mesh=mesh,
        in_specs=(
            P(None, ("branch", "sub")),
            P(None, ("branch", "sub")),
            P(("branch", "sub"), None, None),
            P(("branch", "sub"), None, None),
            P(("branch", "sub"), None, None),
            P(("branch", "sub"), None),
            P(("branch", "sub")),
            P(("branch", "sub"), None),
            P(("branch", "sub")),
            P(("branch", "sub"), None, None, None),
            P("branch", None),
            P("branch"),
            P("branch", None, None, None),
        ),
        out_specs=P(None, ("branch", "sub")),
        check_vma=False,
    )
```

```python
import functools

import jax
import jax.numpy as jnp
from jax import lax
from jax.experimental import pallas as pl
from jax.experimental.pallas import tpu as pltpu
from jax.sharding import PartitionSpec as P

LEAF = 256
RANK = 64
COLS = 64
HERE = 32
NEAR = 5
COUP = 6
BCOUP = 3
REACH = 2
MARGIN = REACH * LEAF
POINTS = HERE * LEAF
PADDED = POINTS + 2 * MARGIN
FEAT = 16

KERNEL_SCALE = 0.03125
DELTA_SQUARED = 0.01

NX, NY = 4, 8
NZ, NC = 8, 2
N_SUB = NX * NY
N_BRANCH = NZ * NC

MESH = pl.DeviceIdType.MESH
F32 = jnp.float32
BF16 = jnp.bfloat16

PAIRS = (2, 6, 11)
FAR = 1024
CLIMB = 16


def dot_nn(a, b, precision=None):
    return lax.dot_general(
        a, b, (((1,), (0,)), ((), ())), precision=precision, preferred_element_type=F32
    )


def dot_nt(a, b, precision=None):
    return lax.dot_general(
        a, b, (((1,), (1,)), ((), ())), precision=precision, preferred_element_type=F32
    )


def halves(x):
    high = x.astype(BF16)
    return high, (x - high.astype(F32)).astype(BF16)


def dot_split(dot, a, b):
    a_high, a_low = halves(a)
    b_high, b_low = halves(b)
    return dot(a_high, b_high) + (dot(a_high, b_low) + dot(a_low, b_high))


def dot_left_split(a, b):
    a_high, a_low = halves(a)
    return dot_nn(a_high, b) + dot_nn(a_low, b)


def packed(x):
    half = x.shape[0] // 2
    return jnp.concatenate([x[:half], x[half:]], axis=1)


def unpacked(x):
    half = x.shape[1] // 2
    return jnp.concatenate([x[:, :half], x[:, half:]], axis=0)


def diagonal_blocks(x):
    return x[:RANK, :RANK] + x[RANK:, RANK:]


def features(coords):
    c = coords.astype(F32)
    x, y, z = c[0:1], c[1:2], c[2:3]
    norm = x * x + y * y + z * z + 0.5 * DELTA_SQUARED
    n1 = norm.astype(BF16).astype(F32)
    n2 = (norm - n1).astype(BF16).astype(F32)
    n3 = norm - n1 - n2
    row = lax.broadcasted_iota(jnp.int32, (FEAT, coords.shape[1]), 0)
    ones = jnp.ones_like(norm)

    def stacked(parts):
        out = jnp.zeros((FEAT, coords.shape[1]), F32)
        for at, part in enumerate(parts):
            out = jnp.where(row == at, part, out)
        return out.astype(BF16)

    source = stacked([x, y, z, n1, n2, n3, ones, ones, ones])
    target = stacked([-2.0 * x, -2.0 * y, -2.0 * z, ones, ones, ones, n1, n2, n3])
    return source, target


def leaf_columns(at):
    return pl.ds(pl.multiple_of(at * LEAF, LEAF), LEAF)


def prepare_features(at, coords, source_feat, source_feat_t, target_feat):
    feat_source, feat_target = features(coords[:, leaf_columns(at)])
    source_feat[:, leaf_columns(at + REACH)] = feat_source
    source_feat_t[leaf_columns(at + REACH), :] = feat_source.astype(F32).T.astype(BF16)
    target_feat[:, leaf_columns(at)] = feat_target


def transpose_features(at, source_feat, source_feat_t):
    block = source_feat[:, leaf_columns(at)].astype(F32)
    source_feat_t[leaf_columns(at), :] = block.T.astype(BF16)


def over_lanes(column):
    return jnp.broadcast_to(column, (column.shape[0], 128))


def eliminate_block(step, ref):
    base = pl.multiple_of(step * 8, 8)
    tiles = [slice(at, at + 128) for at in range(0, ref.shape[1], 128)]
    whole = [ref[:, tile] for tile in tiles]
    rows = [ref[pl.ds(base, 8), tile] for tile in tiles]
    columns = [over_lanes(whole[0][:, j : j + 1]) for j in range(8)]
    heads = [over_lanes(rows[0][:, j : j + 1]) for j in range(8)]
    below = lax.broadcasted_iota(jnp.int32, (RANK, 128), 0) >= base + 8
    sublane = lax.broadcasted_iota(jnp.int32, (8, 128), 0)
    scale = jnp.zeros((8, 128), F32)
    taken = [jnp.zeros((RANK, 128), F32) for _ in tiles]
    for j in range(8):
        pivot = heads[j][j : j + 1, :]
        inverse = 1.0 / pivot
        scale = jnp.where(sublane == j, lax.rsqrt(pivot), scale)
        inside = jnp.where(sublane > j, heads[j] * inverse, 0.0)
        factor = columns[j] * inverse
        for m in range(j + 1, 8):
            entry = heads[m][j : j + 1, :]
            heads[m] = heads[m] - inside * entry
            columns[m] = columns[m] - factor * entry
        for t in range(len(tiles)):
            pivot_row = rows[t][j : j + 1, :]
            rows[t] = rows[t] - inside * pivot_row
            taken[t] = taken[t] + factor * pivot_row
    for t, tile in enumerate(tiles):
        ref[:, tile] = jnp.where(below, whole[t] - taken[t], whole[t])
        ref[pl.ds(base, 8), tile] = rows[t] * scale
    ref[:, 0:128] = pltpu.roll(ref[:, 0:128], 120, 1)


def eliminate(rows):
    sublane = lax.broadcasted_iota(jnp.int32, (8, 128), 0)
    for block in range(RANK // 8):
        lanes = range(8 * block, 8 * block + 8)
        heads = [over_lanes(rows[block][0][:, k : k + 1]) for k in lanes]
        inverses, entries, pivot_rows = [], [], []
        scale = jnp.zeros((8, 128), F32)
        done = rows[block]
        for j in range(8):
            pivot = heads[j][j : j + 1, :]
            inverse = 1.0 / pivot
            scale = jnp.where(sublane == j, lax.rsqrt(pivot), scale)
            inside = jnp.where(sublane > j, heads[j] * inverse, 0.0)
            entry = {m: heads[m][j : j + 1, :] for m in range(j + 1, 8)}
            for m in entry:
                heads[m] = heads[m] - inside * entry[m]
            pivot_row = [tile[j : j + 1, :] for tile in done]
            done = [tile - inside * line for tile, line in zip(done, pivot_row)]
            inverses.append(inverse)
            entries.append(entry)
            pivot_rows.append(pivot_row)
        rows[block] = [tile * scale for tile in done]
        for at in range(block + 1, RANK // 8):
            columns = [over_lanes(rows[at][0][:, k : k + 1]) for k in lanes]
            for j in range(8):
                factor = columns[j] * inverses[j]
                for m, entry in entries[j].items():
                    columns[m] = columns[m] - factor * entry
                rows[at] = [
                    tile - factor * line for tile, line in zip(rows[at], pivot_rows[j])
                ]
    return rows


def climb_leaves(low, high, total, transfer, basis, window, vt_out):
    def lifted(at):
        block = transfer[at].T
        block_high = block.astype(BF16)
        block_low = (block - block_high.astype(F32)).astype(BF16)
        leaf_basis = basis[at]
        return (dot_nn(block_high, leaf_basis) + dot_nn(block_low, leaf_basis)).astype(BF16)

    def climb(it, total):
        points = pl.multiple_of(it * (CLIMB * LEAF), CLIMB * LEAF)
        vt = jnp.concatenate([lifted(it * CLIMB + u) for u in range(CLIMB)], axis=1)
        vt_out[:, pl.ds(points, CLIMB * LEAF)] = vt
        values = window[:, pl.ds(pl.multiple_of(points + MARGIN, LEAF), CLIMB * LEAF)]
        return total + dot_nt(vt, jnp.concatenate([vt, values], axis=0))

    return lax.fori_loop(low // CLIMB, high // CLIMB, climb, total)


def near_start(at, made, source_feat_t, target_feat):
    target = target_feat[:, leaf_columns(at)]
    for shift in range(NEAR):
        distance = dot_nn(source_feat_t[leaf_columns(at + shift), :], target)
        made[shift * LEAF : (shift + 1) * LEAF, :] = lax.rsqrt(distance).astype(BF16)


def near_step(
    at, following, used, made, near_slots, near_count, source_feat_t, target_feat, window, near_out
):
    last = following is None
    target = None if last else target_feat[:, leaf_columns(following)]
    live = near_count[at]
    result = jnp.zeros((COLS, LEAF), F32)
    for shift in range(NEAR):
        weight = jnp.int32(0)
        for slot in range(NEAR):
            weight = weight + jnp.where(
                jnp.logical_and(near_slots[slot, at] == shift, slot < live), 1, 0
            )
        values = window[:, leaf_columns(at + shift)]
        values = values * jnp.full(values.shape, weight.astype(F32)).astype(BF16)
        rows = slice(shift * LEAF, (shift + 1) * LEAF)
        result = result + dot_nn(values, used[rows, :])
        if not last:
            distance = dot_nn(source_feat_t[leaf_columns(following + shift), :], target)
            made[rows, :] = lax.rsqrt(distance).astype(BF16)
    near_out[:, leaf_columns(at)] = result * KERNEL_SCALE


def main_kernel(
    cluster_count,
    branch_count,
    sources,
    coords_hbm,
    basis_hbm,
    transfer_hbm,
    cluster_transfer_hbm,
    near_slots_hbm,
    near_count_hbm,
    cluster_partners_hbm,
    coupling_hbm,
    branch_partners_hbm,
    branch_tiles_hbm,
    near_out,
    vt_out,
    down_out,
    coords,
    basis,
    transfer,
    cluster_transfer,
    near_slots,
    near_count,
    cluster_partners,
    coupling,
    branch_partners,
    branch_tiles,
    window,
    source_feat,
    target_feat,
    source_feat_t,
    all_transfer,
    all_gram,
    all_pairs,
    all_share,
    all_ortho,
    all_branch,
    right,
    blocks_even,
    blocks_odd,
    local_sems,
    halo_send,
    halo_recv,
    send_sems,
    recv_sems,
):
    branch = lax.axis_index("branch")
    sub = lax.axis_index("sub")
    sx, sy = sub % NX, sub // NX
    bz, bc = branch // NC, branch % NC

    half, half_points = HERE // 2, POINTS // 2
    pieces = []
    for part in range(2):
        leaves = pl.ds(part * half, half)
        pieces += [
            (transfer_hbm.at[leaves], transfer.at[leaves]),
            (basis_hbm.at[leaves], basis.at[leaves]),
            (
                sources.at[:, pl.ds(part * half_points, half_points)],
                window.at[:, pl.ds(MARGIN + part * half_points, half_points)],
            ),
        ]
    pieces += [
        (cluster_transfer_hbm, cluster_transfer),
        (coords_hbm, coords),
        (near_slots_hbm, near_slots),
        (near_count_hbm, near_count),
        (cluster_partners_hbm, cluster_partners),
        (coupling_hbm, coupling),
        (branch_partners_hbm, branch_partners),
        (branch_tiles_hbm, branch_tiles),
    ]
    loads = [
        pltpu.make_async_copy(src, dst, local_sems.at[at])
        for at, (src, dst) in enumerate(pieces)
    ]
    for load in loads:
        load.start()

    at_x = [(sx + d) % NX for d in range(NX)]
    at_y = [(sy + d) % NY * NX for d in range(NY)]
    at_z = [(bz + d) % NZ * NC for d in range(NZ)]
    at_c = [(bc + d) % NC for d in range(NC)]
    peers_x = [(branch, at_y[0] + at_x[d]) for d in range(NX)]
    peers_y = [(branch, at_y[d] + at_x[0]) for d in range(NY)]
    peers_z = [(at_z[d] + at_c[0], sub) for d in range(NZ)]
    peer_core = (at_z[0] + at_c[1], sub)

    here = branch * N_SUB + sub
    total = N_BRANCH * N_SUB
    after = (here + 1) % total
    before = (here + total - 1) % total
    after_id = (after // N_SUB, after % N_SUB)
    before_id = (before // N_SUB, before % N_SUB)

    barrier = pltpu.get_barrier_semaphore()
    greeted = peers_z[1:] + peers_y[1:] + peers_x[1:] + [peer_core, after_id, before_id]
    for device in greeted:
        pl.semaphore_signal(barrier, inc=1, device_id=device, device_id_type=MESH)

    def gather_copy(src, dst, slot, device):
        return pltpu.make_async_remote_copy(
            src_ref=src,
            dst_ref=dst,
            send_sem=send_sems.at[slot],
            recv_sem=recv_sems.at[slot],
            device_id=device,
            device_id_type=MESH,
        )

    def all_copies(buffer, slot, count, first=1):
        others = buffer.at[pl.ds(first, count - first)]
        return gather_copy(others, others, slot, peer_core)

    def start_ring(buffer, slot, peers, width=1):
        size = len(peers)
        for d in sorted(range(1, size), key=lambda d: -min(d, size - d)):
            gather_copy(
                buffer.at[pl.ds(0, width)],
                buffer.at[pl.ds(d * width, width)],
                slot,
                peers[d],
            ).start()

    def halo_copy(src, dst, at, device):
        return pltpu.make_async_remote_copy(
            src_ref=src,
            dst_ref=dst,
            send_sem=halo_send.at[at],
            recv_sem=halo_recv.at[at],
            device_id=device,
            device_id_type=MESH,
        )

    low, high = pl.ds(0, MARGIN), pl.ds(MARGIN + POINTS, MARGIN)
    halos = [
        halo_copy(
            sources.at[:, pl.ds(POINTS - MARGIN, MARGIN)], window.at[:, low], 0, after_id
        ),
        halo_copy(sources.at[:, pl.ds(0, MARGIN)], window.at[:, high], 1, before_id),
        halo_copy(
            source_feat.at[:, pl.ds(POINTS, MARGIN)], source_feat.at[:, low], 2, after_id
        ),
        halo_copy(
            source_feat.at[:, pl.ds(MARGIN, MARGIN)], source_feat.at[:, high], 3, before_id
        ),
    ]

    climb = functools.partial(
        climb_leaves, transfer=transfer, basis=basis, window=window, vt_out=vt_out
    )
    for load in loads[:3]:
        load.wait()
    gram_up = climb(0, half, jnp.zeros((RANK, 2 * RANK), F32))

    loads[6].wait()
    own_transfer = cluster_transfer[0]
    all_transfer[0] = packed(own_transfer).astype(BF16)
    own_transfer_t = own_transfer.T.astype(BF16)
    pl.semaphore_wait(barrier, len(greeted))
    start_ring(all_transfer, 0, peers_x)
    halos[0].start()
    halos[1].start()

    for load in loads[3:6]:
        load.wait()
    gram_up = climb(half, HERE, gram_up)

    row = lax.broadcasted_iota(jnp.int32, (RANK, 128), 0)
    lane = lax.broadcasted_iota(jnp.int32, (RANK, 128), 1)
    identity = jnp.where(row == lane, 1.0, 0.0)
    rows = eliminate(
        [[part[8 * r : 8 * r + 8, :] for part in (gram_up, identity)] for r in range(RANK // 8)]
    )
    ortho_t = jnp.concatenate([tiles[0][:, RANK:] for tiles in rows], axis=0)
    inverse = jnp.concatenate([tiles[1][:, :RANK] for tiles in rows], axis=0)
    share = dot_nn(own_transfer_t, ortho_t.astype(BF16))
    all_pairs[0] = jnp.concatenate([packed(share), packed(ortho_t)], axis=0).astype(BF16)
    start_ring(all_pairs, 1, peers_x)

    all_copies(all_transfer, 0, NX).wait_recv()
    stack = all_transfer[...].reshape(NX * RANK // 2, 2 * RANK)
    partial_gram = diagonal_blocks(dot_nn(stack.astype(F32).T.astype(BF16), stack))
    all_gram[0] = packed(partial_gram).astype(BF16)
    start_ring(all_gram, 3, peers_y)

    near_of = dict(
        near_slots=near_slots,
        near_count=near_count,
        source_feat_t=source_feat_t,
        target_feat=target_feat,
        window=window,
        near_out=near_out,
    )

    def prepare(at):
        prepare_features(at, coords, source_feat, source_feat_t, target_feat)

    for load in loads[7:]:
        load.wait()
    for at in (0, 1, HERE - 2, HERE - 1):
        prepare(at)
    halos[2].start()
    halos[3].start()
    for at in range(REACH, 2 * REACH + 2):
        prepare(at)
    near_start(REACH, blocks_even, source_feat_t, target_feat)

    def near_pair(at, following):
        for step, used, made in ((0, blocks_even, blocks_odd), (1, blocks_odd, blocks_even)):
            prepare(jnp.minimum(at + step + 2 * REACH, HERE - REACH - 1))
            near_step(at + step, following if step else at + 1, used, made, **near_of)

    inverse_t = inverse.T
    all_copies(all_pairs, 1, NX).wait_recv()
    pairs = all_pairs[...]
    all_share[0] = jnp.sum(pairs[:, : RANK // 2].astype(F32), axis=0).astype(BF16)
    start_ring(all_share, 4, peers_y)
    all_ortho[0:NX] = pairs[:, RANK // 2 :]
    start_ring(all_ortho, 5, peers_y, NX)

    def plain_pairs(first, last):
        @pl.loop(first, last)
        def _(it):
            near_pair(REACH + 2 * it, REACH + 2 * it + 2)

    plain_pairs(0, PAIRS[0])
    all_copies(all_gram, 3, NY).wait_recv()
    branch_gram = unpacked(jnp.sum(all_gram[...].astype(F32), axis=0))
    right[...] = jnp.concatenate([branch_gram, identity[:, :RANK]], axis=1)

    @pl.loop(PAIRS[0], PAIRS[1])
    def _(it):
        near_pair(REACH + 2 * it, REACH + 2 * it + 2)
        blocks = RANK // 8 // (PAIRS[1] - PAIRS[0])
        for j in range(blocks):
            eliminate_block((it - PAIRS[0]) * blocks + j, right)

    branch_inverse = right[:, 0:RANK]

    all_copies(all_share, 4, NY).wait_recv()
    branch_up_t = unpacked(jnp.sum(all_share[...].astype(F32), axis=0))
    branch_ortho_t = dot_split(dot_nn, branch_inverse, branch_up_t)
    all_branch[0] = packed(branch_ortho_t).astype(BF16)
    start_ring(all_branch, 2, peers_z)

    cluster_map = dot_split(dot_nt, inverse_t, coupling[0].reshape(COUP * RANK, RANK))
    handed = dot_split(dot_nt, dot_split(dot_nn, inverse_t, own_transfer), branch_inverse)
    branch_map = dot_split(dot_nt, handed, branch_tiles[0].reshape(BCOUP * RANK, RANK))

    plain_pairs(PAIRS[1], PAIRS[2])

    all_copies(all_branch, 2, NZ).wait_recv()
    gather_copy(
        all_branch.at[pl.ds(0, NZ)], all_branch.at[pl.ds(NZ, NZ)], 6, peer_core
    ).start()

    plain_pairs(PAIRS[2], (HERE - 2 * REACH) // 2 - 1)
    for copy in halos:
        copy.wait_recv()
    keep_low = jnp.where(here == 0, 0.0, 1.0)
    keep_high = jnp.where(here == total - 1, 0.0, 1.0)
    for columns, keep in ((slice(0, MARGIN), keep_low), (slice(MARGIN + POINTS, PADDED), keep_high)):
        edge = window[:, columns]
        window[:, columns] = edge * jnp.full(edge.shape, keep).astype(BF16)
    for at in (0, 1, HERE + REACH, HERE + REACH + 1):
        transpose_features(at, source_feat, source_feat_t)
    edges = (HERE - REACH - 2, HERE - REACH - 1, 0, 1, HERE - 2, HERE - 1, None)
    for it in range(6):
        used, made = ((blocks_even, blocks_odd), (blocks_odd, blocks_even))[it % 2]
        near_step(edges[it], edges[it + 1], used, made, **near_of)

    all_copies(all_ortho, 5, N_SUB, NX).wait_recv()
    picked = []
    for k in range(COUP):
        partner = cluster_partners[0, k]
        slot = ((sy - partner // NX + NY) % NY) * NX + (sx - partner % NX + NX) % NX
        alive = jnp.where(k < cluster_count[0], 1.0, 0.0)
        picked.append((unpacked(all_ortho[slot].astype(F32)) * alive).astype(BF16))
    down_t = dot_left_split(cluster_map, jnp.concatenate(picked, axis=0))

    all_copies(all_branch, 6, 2 * NZ, NZ).wait_recv()
    picked = []
    for k in range(BCOUP):
        partner = branch_partners[0, k]
        slot = ((bc - partner % NC + NC) % NC) * NZ + (bz - partner // NC + NZ) % NZ
        alive = jnp.where(k < branch_count[0], 1.0, 0.0)
        picked.append((unpacked(all_branch[slot].astype(F32)) * alive).astype(BF16))
    down_t = down_t + dot_left_split(branch_map, jnp.concatenate(picked, axis=0))
    down_out[...] = down_t.T

    for copy in halos:
        copy.wait_send()
    all_copies(all_transfer, 0, NX).wait_send()
    all_copies(all_pairs, 1, NX).wait_send()
    all_copies(all_branch, 2, NZ).wait_send()
    all_copies(all_gram, 3, NY).wait_send()
    all_copies(all_share, 4, NY).wait_send()
    all_copies(all_ortho, 5, N_SUB, NX).wait_send()
    all_copies(all_branch, 6, 2 * NZ, NZ).wait_send()


def far_kernel(near, vt, down, out, total, sems):
    high = down[...].astype(BF16)
    low = (down[...] - high.astype(F32)).astype(BF16)
    copies = []
    for at in range(POINTS // FAR):
        columns = slice(at * FAR, (at + 1) * FAR)
        total[:, columns] = (
            near[:, columns] + dot_nn(high, vt[:, columns]) + dot_nn(low, vt[:, columns])
        )
        copies.append(
            pltpu.make_async_copy(total.at[:, columns], out.at[:, columns], sems.at[at])
        )
        copies[-1].start()
    for copy in copies:
        copy.wait()


def shards(
    sources,
    coords,
    leaf_basis,
    leaf_transfer,
    cluster_transfer,
    near_slots,
    near_count,
    cluster_partners,
    cluster_count,
    cluster_coupling,
    branch_partners,
    branch_count,
    branch_coupling_tiles,
):
    vmem = pl.BlockSpec(memory_space=pltpu.VMEM)
    smem = pl.BlockSpec(memory_space=pltpu.SMEM)
    hbm = pl.BlockSpec(memory_space=pltpu.HBM)
    near, vt, down = pl.pallas_call(
        main_kernel,
        out_shape=(
            jax.ShapeDtypeStruct((COLS, POINTS), F32),
            jax.ShapeDtypeStruct((RANK, POINTS), BF16),
            jax.ShapeDtypeStruct((COLS, RANK), F32),
        ),
        in_specs=[smem] * 2 + [hbm] * 11,
        out_specs=(vmem, vmem, vmem),
        scratch_shapes=[
            pltpu.VMEM((3, POINTS), BF16),
            pltpu.VMEM((HERE, RANK, LEAF), BF16),
            pltpu.VMEM((HERE, RANK, RANK), F32),
            pltpu.VMEM((1, RANK, RANK), F32),
            pltpu.SMEM((NEAR, HERE), jnp.int32),
            pltpu.SMEM((HERE,), jnp.int32),
            pltpu.SMEM((1, COUP), jnp.int32),
            pltpu.VMEM((1, COUP, RANK, RANK), F32),
            pltpu.SMEM((1, BCOUP), jnp.int32),
            pltpu.VMEM((1, BCOUP, RANK, RANK), F32),
            pltpu.VMEM((COLS, PADDED), BF16),
            pltpu.VMEM((FEAT, PADDED), BF16),
            pltpu.VMEM((FEAT, POINTS), BF16),
            pltpu.VMEM((PADDED, FEAT), BF16),
            pltpu.VMEM((NX, RANK // 2, 2 * RANK), BF16),
            pltpu.VMEM((NY, RANK // 2, 2 * RANK), BF16),
            pltpu.VMEM((NX, RANK, 2 * RANK), BF16),
            pltpu.VMEM((NY, RANK // 2, 2 * RANK), BF16),
            pltpu.VMEM((N_SUB, RANK // 2, 2 * RANK), BF16),
            pltpu.VMEM((N_BRANCH, RANK // 2, 2 * RANK), BF16),
            pltpu.VMEM((RANK, 128), F32),
            pltpu.VMEM((NEAR * LEAF, LEAF), BF16),
            pltpu.VMEM((NEAR * LEAF, LEAF), BF16),
            pltpu.SemaphoreType.DMA((14,)),
            pltpu.SemaphoreType.DMA((4,)),
            pltpu.SemaphoreType.DMA((4,)),
            pltpu.SemaphoreType.DMA((7,)),
            pltpu.SemaphoreType.DMA((7,)),
        ],
        compiler_params=pltpu.CompilerParams(
            collective_id=0, has_side_effects=True, vmem_limit_bytes=40 * 2**20
        ),
        name="h2_main",
    )(
        cluster_count,
        branch_count,
        *(
            pltpu.with_memory_space_constraint(operand, pltpu.HBM)
            for operand in (
                sources,
                coords,
                leaf_basis,
                leaf_transfer,
                cluster_transfer,
                near_slots.T,
                near_count,
                cluster_partners,
                cluster_coupling,
                branch_partners,
                branch_coupling_tiles,
            )
        )
    )
    return pl.pallas_call(
        far_kernel,
        out_shape=jax.ShapeDtypeStruct((COLS, POINTS), F32),
        in_specs=[vmem] * 3,
        out_specs=hbm,
        scratch_shapes=[
            pltpu.VMEM((COLS, POINTS), F32),
            pltpu.SemaphoreType.DMA((POINTS // FAR,)),
        ],
        compiler_params=pltpu.CompilerParams(vmem_limit_bytes=32 * 2**20),
        name="h2_far",
    )(near, vt, down)


def solution(mesh):
    return jax.shard_map(
        shards,
        mesh=mesh,
        in_specs=(
            P(None, ("branch", "sub")),
            P(None, ("branch", "sub")),
            P(("branch", "sub"), None, None),
            P(("branch", "sub"), None, None),
            P(("branch", "sub"), None, None),
            P(("branch", "sub"), None),
            P(("branch", "sub")),
            P(("branch", "sub"), None),
            P(("branch", "sub")),
            P(("branch", "sub"), None, None, None),
            P("branch", None),
            P("branch"),
            P("branch", None, None, None),
        ),
        out_specs=P(None, ("branch", "sub")),
        check_vma=False,
    )
```

```python
import functools

import jax
import jax.numpy as jnp
from jax import lax
from jax.experimental import pallas as pl
from jax.experimental.pallas import tpu as pltpu
from jax.sharding import PartitionSpec as P

LEAF = 256
RANK = 64
COLS = 64
HERE = 32
NEAR = 5
COUP = 6
BCOUP = 3
REACH = 2
MARGIN = REACH * LEAF
POINTS = HERE * LEAF
PADDED = POINTS + 2 * MARGIN
FEAT = 16

KERNEL_SCALE = 0.03125
DELTA_SQUARED = 0.01

NX, NY = 4, 8
NZ, NC = 8, 2
N_SUB = NX * NY
N_BRANCH = NZ * NC

MESH = pl.DeviceIdType.MESH
F32 = jnp.float32
BF16 = jnp.bfloat16

PAIRS = (0, 2, 6, 12)
FAR = 1024
CLIMB = 16


def dot_nn(a, b, precision=None):
    return lax.dot_general(
        a, b, (((1,), (0,)), ((), ())), precision=precision, preferred_element_type=F32
    )


def dot_nt(a, b, precision=None):
    return lax.dot_general(
        a, b, (((1,), (1,)), ((), ())), precision=precision, preferred_element_type=F32
    )


def halves(x):
    high = x.astype(BF16)
    return high, (x - high.astype(F32)).astype(BF16)


def dot_split(dot, a, b):
    a_high, a_low = halves(a)
    b_high, b_low = halves(b)
    return dot(a_high, b_high) + (dot(a_high, b_low) + dot(a_low, b_high))


def dot_left_split(a, b):
    a_high, a_low = halves(a)
    return dot_nn(a_high, b) + dot_nn(a_low, b)


def packed(x):
    half = x.shape[0] // 2
    return jnp.concatenate([x[:half], x[half:]], axis=1)


def unpacked(x):
    half = x.shape[1] // 2
    return jnp.concatenate([x[:, :half], x[:, half:]], axis=0)


def diagonal_blocks(x):
    return x[:RANK, :RANK] + x[RANK:, RANK:]


def features(coords):
    c = coords.astype(F32)
    x, y, z = c[0:1], c[1:2], c[2:3]
    norm = x * x + y * y + z * z + 0.5 * DELTA_SQUARED
    n1 = norm.astype(BF16).astype(F32)
    n2 = (norm - n1).astype(BF16).astype(F32)
    n3 = norm - n1 - n2
    row = lax.broadcasted_iota(jnp.int32, (FEAT // 2, coords.shape[1]), 0)
    point = jnp.zeros((FEAT // 2, coords.shape[1]), F32)
    for at, part in enumerate((x, y, z, n1, n2, n3)):
        point = jnp.where(row == at, part, point)
    is_norm = jnp.logical_and(row >= 3, row < 6)
    ones = jnp.where(is_norm, 1.0, 0.0)
    source = jnp.concatenate([point, ones], axis=0)
    target = jnp.concatenate(
        [jnp.where(is_norm, 1.0, -2.0 * point), jnp.where(is_norm, point, 0.0)], axis=0
    )
    return source, target.astype(BF16)


def leaf_columns(at):
    return pl.ds(pl.multiple_of(at * LEAF, LEAF), LEAF)


def prepare_features(at, coords, source_feat, source_feat_t, target_feat):
    feat_source, feat_target = features(coords[:, leaf_columns(at)])
    source_feat[:, leaf_columns(at + REACH)] = feat_source.astype(BF16)
    source_feat_t[leaf_columns(at + REACH), :] = feat_source.T.astype(BF16)
    target_feat[:, leaf_columns(at)] = feat_target


def transpose_features(at, source_feat, source_feat_t):
    block = source_feat[:, leaf_columns(at)].astype(F32)
    source_feat_t[leaf_columns(at), :] = block.T.astype(BF16)


def over_lanes(column):
    return jnp.broadcast_to(column, (column.shape[0], 128))


def eliminate_block(step, ref):
    base = pl.multiple_of(step * 8, 8)
    tiles = [slice(at, at + 128) for at in range(0, ref.shape[1], 128)]
    whole = [ref[:, tile] for tile in tiles]
    rows = [ref[pl.ds(base, 8), tile] for tile in tiles]
    columns = [over_lanes(whole[0][:, j : j + 1]) for j in range(8)]
    heads = [over_lanes(rows[0][:, j : j + 1]) for j in range(8)]
    below = lax.broadcasted_iota(jnp.int32, (RANK, 128), 0) >= base + 8
    sublane = lax.broadcasted_iota(jnp.int32, (8, 128), 0)
    scale = jnp.zeros((8, 128), F32)
    taken = [jnp.zeros((RANK, 128), F32) for _ in tiles]
    for j in range(8):
        pivot = heads[j][j : j + 1, :]
        inverse = 1.0 / pivot
        scale = jnp.where(sublane == j, lax.rsqrt(pivot), scale)
        inside = jnp.where(sublane > j, heads[j] * inverse, 0.0)
        factor = columns[j] * inverse
        for m in range(j + 1, 8):
            entry = heads[m][j : j + 1, :]
            heads[m] = heads[m] - inside * entry
            columns[m] = columns[m] - factor * entry
        for t in range(len(tiles)):
            pivot_row = rows[t][j : j + 1, :]
            rows[t] = rows[t] - inside * pivot_row
            taken[t] = taken[t] + factor * pivot_row
    for t, tile in enumerate(tiles):
        ref[:, tile] = jnp.where(below, whole[t] - taken[t], whole[t])
        ref[pl.ds(base, 8), tile] = rows[t] * scale
    ref[:, 0:128] = pltpu.roll(ref[:, 0:128], 120, 1)


def eliminate(rows):
    sublane = lax.broadcasted_iota(jnp.int32, (8, 128), 0)
    for block in range(RANK // 8):
        lanes = range(8 * block, 8 * block + 8)
        heads = [over_lanes(rows[block][0][:, k : k + 1]) for k in lanes]
        inverses, entries, pivot_rows = [], [], []
        scale = jnp.zeros((8, 128), F32)
        done = rows[block]
        for j in range(8):
            pivot = heads[j][j : j + 1, :]
            inverse = 1.0 / pivot
            scale = jnp.where(sublane == j, lax.rsqrt(pivot), scale)
            inside = jnp.where(sublane > j, heads[j] * inverse, 0.0)
            entry = {m: heads[m][j : j + 1, :] for m in range(j + 1, 8)}
            for m in entry:
                heads[m] = heads[m] - inside * entry[m]
            pivot_row = [tile[j : j + 1, :] for tile in done]
            done = [tile - inside * line for tile, line in zip(done, pivot_row)]
            inverses.append(inverse)
            entries.append(entry)
            pivot_rows.append(pivot_row)
        rows[block] = [tile * scale for tile in done]
        for at in range(block + 1, RANK // 8):
            columns = [over_lanes(rows[at][0][:, k : k + 1]) for k in lanes]
            for j in range(8):
                factor = columns[j] * inverses[j]
                for m, entry in entries[j].items():
                    columns[m] = columns[m] - factor * entry
                rows[at] = [
                    tile - factor * line for tile, line in zip(rows[at], pivot_rows[j])
                ]
    return rows


def climb_leaves(low, high, total, transfer, basis, window, vt_out):
    def lifted(at):
        block = transfer[at].T
        block_high = block.astype(BF16)
        block_low = (block - block_high.astype(F32)).astype(BF16)
        leaf_basis = basis[at]
        return (dot_nn(block_high, leaf_basis) + dot_nn(block_low, leaf_basis)).astype(BF16)

    def climb(it, total):
        points = pl.multiple_of(it * (CLIMB * LEAF), CLIMB * LEAF)
        vt = jnp.concatenate([lifted(it * CLIMB + u) for u in range(CLIMB)], axis=1)
        vt_out[:, pl.ds(points, CLIMB * LEAF)] = vt
        values = window[:, pl.ds(pl.multiple_of(points + MARGIN, LEAF), CLIMB * LEAF)]
        return total + dot_nt(vt, jnp.concatenate([vt, values], axis=0))

    return lax.fori_loop(low // CLIMB, high // CLIMB, climb, total)


def near_start(at, made, source_feat_t, target_feat):
    target = target_feat[:, leaf_columns(at)]
    for shift in range(NEAR):
        distance = dot_nn(source_feat_t[leaf_columns(at + shift), :], target)
        made[shift * LEAF : (shift + 1) * LEAF, :] = lax.rsqrt(distance).astype(BF16)


def near_step(
    at, following, used, made, near_slots, near_count, source_feat_t, target_feat, window, near_out
):
    last = following is None
    target = None if last else target_feat[:, leaf_columns(following)]
    live = near_count[at]
    result = jnp.zeros((COLS, LEAF), F32)
    for shift in range(NEAR):
        weight = jnp.int32(0)
        for slot in range(NEAR):
            weight = weight + jnp.where(
                jnp.logical_and(near_slots[slot, at] == shift, slot < live), 1, 0
            )
        values = window[:, leaf_columns(at + shift)]
        values = values * jnp.full(values.shape, weight.astype(F32)).astype(BF16)
        rows = slice(shift * LEAF, (shift + 1) * LEAF)
        result = result + dot_nn(values, used[rows, :])
        if not last:
            distance = dot_nn(source_feat_t[leaf_columns(following + shift), :], target)
            made[rows, :] = lax.rsqrt(distance).astype(BF16)
    near_out[:, leaf_columns(at)] = result * KERNEL_SCALE


def main_kernel(
    cluster_count,
    branch_count,
    sources,
    coords_hbm,
    basis_hbm,
    transfer_hbm,
    cluster_transfer_hbm,
    near_slots_hbm,
    near_count_hbm,
    cluster_partners_hbm,
    coupling_hbm,
    branch_partners_hbm,
    branch_tiles_hbm,
    near_out,
    vt_out,
    down_out,
    coords,
    basis,
    transfer,
    cluster_transfer,
    near_slots,
    near_count,
    cluster_partners,
    coupling,
    branch_partners,
    branch_tiles,
    window,
    source_feat,
    target_feat,
    source_feat_t,
    all_transfer,
    all_gram,
    all_pairs,
    all_share,
    all_ortho,
    all_branch,
    right,
    blocks_even,
    blocks_odd,
    local_sems,
    halo_send,
    halo_recv,
    send_sems,
    recv_sems,
):
    branch = lax.axis_index("branch")
    sub = lax.axis_index("sub")
    sx, sy = sub % NX, sub // NX
    bz, bc = branch // NC, branch % NC

    half, half_points = HERE // 2, POINTS // 2
    pieces = []
    for part in range(2):
        leaves = pl.ds(part * half, half)
        pieces += [
            (transfer_hbm.at[leaves], transfer.at[leaves]),
            (basis_hbm.at[leaves], basis.at[leaves]),
            (
                sources.at[:, pl.ds(part * half_points, half_points)],
                window.at[:, pl.ds(MARGIN + part * half_points, half_points)],
            ),
        ]
    pieces += [
        (cluster_transfer_hbm, cluster_transfer),
        (coords_hbm, coords),
        (near_slots_hbm, near_slots),
        (near_count_hbm, near_count),
        (cluster_partners_hbm, cluster_partners),
        (coupling_hbm, coupling),
        (branch_partners_hbm, branch_partners),
        (branch_tiles_hbm, branch_tiles),
    ]
    loads = [
        pltpu.make_async_copy(src, dst, local_sems.at[at])
        for at, (src, dst) in enumerate(pieces)
    ]
    for load in loads:
        load.start()

    at_x = [(sx + d) % NX for d in range(NX)]
    at_y = [(sy + d) % NY * NX for d in range(NY)]
    at_z = [(bz + d) % NZ * NC for d in range(NZ)]
    at_c = [(bc + d) % NC for d in range(NC)]
    peers_x = [(branch, at_y[0] + at_x[d]) for d in range(NX)]
    peers_y = [(branch, at_y[d] + at_x[0]) for d in range(NY)]
    peers_z = [(at_z[d] + at_c[0], sub) for d in range(NZ)]
    peer_core = (at_z[0] + at_c[1], sub)

    here = branch * N_SUB + sub
    total = N_BRANCH * N_SUB
    after = (here + 1) % total
    before = (here + total - 1) % total
    after_id = (after // N_SUB, after % N_SUB)
    before_id = (before // N_SUB, before % N_SUB)

    barrier = pltpu.get_barrier_semaphore()
    greeted = peers_z[1:] + peers_y[1:] + peers_x[1:] + [peer_core, after_id, before_id]
    for device in greeted:
        pl.semaphore_signal(barrier, inc=1, device_id=device, device_id_type=MESH)

    def gather_copy(src, dst, slot, device):
        return pltpu.make_async_remote_copy(
            src_ref=src,
            dst_ref=dst,
            send_sem=send_sems.at[slot],
            recv_sem=recv_sems.at[slot],
            device_id=device,
            device_id_type=MESH,
        )

    def all_copies(buffer, slot, count, first=1):
        others = buffer.at[pl.ds(first, count - first)]
        return gather_copy(others, others, slot, peer_core)

    def start_ring(buffer, slot, peers, width=1):
        size = len(peers)
        for d in sorted(range(1, size), key=lambda d: -min(d, size - d)):
            gather_copy(
                buffer.at[pl.ds(0, width)],
                buffer.at[pl.ds(d * width, width)],
                slot,
                peers[d],
            ).start()

    def halo_copy(src, dst, at, device):
        return pltpu.make_async_remote_copy(
            src_ref=src,
            dst_ref=dst,
            send_sem=halo_send.at[at],
            recv_sem=halo_recv.at[at],
            device_id=device,
            device_id_type=MESH,
        )

    low, high = pl.ds(0, MARGIN), pl.ds(MARGIN + POINTS, MARGIN)
    halos = [
        halo_copy(
            sources.at[:, pl.ds(POINTS - MARGIN, MARGIN)], window.at[:, low], 0, after_id
        ),
        halo_copy(sources.at[:, pl.ds(0, MARGIN)], window.at[:, high], 1, before_id),
        halo_copy(
            source_feat.at[:, pl.ds(POINTS, MARGIN)], source_feat.at[:, low], 2, after_id
        ),
        halo_copy(
            source_feat.at[:, pl.ds(MARGIN, MARGIN)], source_feat.at[:, high], 3, before_id
        ),
    ]

    climb = functools.partial(
        climb_leaves, transfer=transfer, basis=basis, window=window, vt_out=vt_out
    )
    for load in loads[:3]:
        load.wait()
    gram_up = climb(0, half, jnp.zeros((RANK, 2 * RANK), F32))

    loads[6].wait()
    own_transfer = cluster_transfer[0]
    all_transfer[0] = packed(own_transfer).astype(BF16)
    own_transfer_t = own_transfer.T.astype(BF16)
    pl.semaphore_wait(barrier, len(greeted))
    start_ring(all_transfer, 0, peers_x)
    halos[0].start()
    halos[1].start()

    for load in loads[3:6]:
        load.wait()
    gram_up = climb(half, HERE, gram_up)

    row = lax.broadcasted_iota(jnp.int32, (RANK, 128), 0)
    lane = lax.broadcasted_iota(jnp.int32, (RANK, 128), 1)
    identity = jnp.where(row == lane, 1.0, 0.0)
    rows = eliminate(
        [[part[8 * r : 8 * r + 8, :] for part in (gram_up, identity)] for r in range(RANK // 8)]
    )
    ortho_t = jnp.concatenate([tiles[0][:, RANK:] for tiles in rows], axis=0)
    inverse = jnp.concatenate([tiles[1][:, :RANK] for tiles in rows], axis=0)
    share = dot_nn(own_transfer_t, ortho_t.astype(BF16))
    all_pairs[0] = jnp.concatenate([packed(share), packed(ortho_t)], axis=0).astype(BF16)
    start_ring(all_pairs, 1, peers_x)

    all_copies(all_transfer, 0, NX).wait_recv()
    stack = all_transfer[...].reshape(NX * RANK // 2, 2 * RANK)
    partial_gram = diagonal_blocks(dot_nn(stack.astype(F32).T.astype(BF16), stack))
    all_gram[0] = packed(partial_gram).astype(BF16)
    start_ring(all_gram, 3, peers_y)

    near_of = dict(
        near_slots=near_slots,
        near_count=near_count,
        source_feat_t=source_feat_t,
        target_feat=target_feat,
        window=window,
        near_out=near_out,
    )

    def prepare(at):
        prepare_features(at, coords, source_feat, source_feat_t, target_feat)

    for load in loads[7:]:
        load.wait()
    for at in (0, 1, HERE - 2, HERE - 1):
        prepare(at)
    halos[2].start()
    halos[3].start()
    for at in range(REACH, 2 * REACH + 2):
        prepare(at)
    near_start(REACH, blocks_even, source_feat_t, target_feat)

    def near_pair(at, following):
        for step, used, made in ((0, blocks_even, blocks_odd), (1, blocks_odd, blocks_even)):
            prepare(jnp.minimum(at + step + 2 * REACH, HERE - REACH - 1))
            near_step(at + step, following if step else at + 1, used, made, **near_of)

    def plain_pairs(first, last):
        @pl.loop(first, last, unroll=2 - (last - first) % 2)
        def _(it):
            near_pair(REACH + 2 * it, REACH + 2 * it + 2)

    plain_pairs(0, PAIRS[0])
    inverse_t = inverse.T
    all_copies(all_pairs, 1, NX).wait_recv()
    pairs = all_pairs[...]
    all_share[0] = jnp.sum(pairs[:, : RANK // 2].astype(F32), axis=0).astype(BF16)
    start_ring(all_share, 4, peers_y)
    all_ortho[0:NX] = pairs[:, RANK // 2 :]
    start_ring(all_ortho, 5, peers_y, NX)

    plain_pairs(PAIRS[0], PAIRS[1])
    all_copies(all_gram, 3, NY).wait_recv()
    branch_gram = unpacked(jnp.sum(all_gram[...].astype(F32), axis=0))
    right[...] = jnp.concatenate([branch_gram, identity[:, :RANK]], axis=1)

    @pl.loop(PAIRS[1], PAIRS[2], unroll=2)
    def _(it):
        near_pair(REACH + 2 * it, REACH + 2 * it + 2)
        blocks = RANK // 8 // (PAIRS[2] - PAIRS[1])
        for j in range(blocks):
            eliminate_block((it - PAIRS[1]) * blocks + j, right)

    branch_inverse = right[:, 0:RANK]

    all_copies(all_share, 4, NY).wait_recv()
    branch_up_t = unpacked(jnp.sum(all_share[...].astype(F32), axis=0))
    branch_ortho_t = dot_split(dot_nn, branch_inverse, branch_up_t)
    all_branch[0] = packed(branch_ortho_t).astype(BF16)
    start_ring(all_branch, 2, peers_z)

    cluster_map = dot_split(dot_nt, inverse_t, coupling[0].reshape(COUP * RANK, RANK))
    handed = dot_split(dot_nt, dot_split(dot_nn, inverse_t, own_transfer), branch_inverse)
    branch_map = dot_split(dot_nt, handed, branch_tiles[0].reshape(BCOUP * RANK, RANK))

    plain_pairs(PAIRS[2], PAIRS[3])

    all_copies(all_branch, 2, NZ).wait_recv()
    gather_copy(
        all_branch.at[pl.ds(0, NZ)], all_branch.at[pl.ds(NZ, NZ)], 6, peer_core
    ).start()

    plain_pairs(PAIRS[3], (HERE - 2 * REACH) // 2 - 1)
    for copy in halos:
        copy.wait_recv()
    keep_low = jnp.where(here == 0, 0.0, 1.0)
    keep_high = jnp.where(here == total - 1, 0.0, 1.0)
    for columns, keep in ((slice(0, MARGIN), keep_low), (slice(MARGIN + POINTS, PADDED), keep_high)):
        edge = window[:, columns]
        window[:, columns] = edge * jnp.full(edge.shape, keep).astype(BF16)
    for at in (0, 1, HERE + REACH, HERE + REACH + 1):
        transpose_features(at, source_feat, source_feat_t)
    edges = (HERE - REACH - 2, HERE - REACH - 1, 0, 1, HERE - 2, HERE - 1, None)
    for it in range(6):
        used, made = ((blocks_even, blocks_odd), (blocks_odd, blocks_even))[it % 2]
        near_step(edges[it], edges[it + 1], used, made, **near_of)

    all_copies(all_ortho, 5, N_SUB, NX).wait_recv()
    picked = []
    for k in range(COUP):
        partner = cluster_partners[0, k]
        slot = ((sy - partner // NX + NY) % NY) * NX + (sx - partner % NX + NX) % NX
        alive = jnp.where(k < cluster_count[0], 1.0, 0.0)
        picked.append((unpacked(all_ortho[slot].astype(F32)) * alive).astype(BF16))
    down_t = dot_left_split(cluster_map, jnp.concatenate(picked, axis=0))

    all_copies(all_branch, 6, 2 * NZ, NZ).wait_recv()
    picked = []
    for k in range(BCOUP):
        partner = branch_partners[0, k]
        slot = ((bc - partner % NC + NC) % NC) * NZ + (bz - partner // NC + NZ) % NZ
        alive = jnp.where(k < branch_count[0], 1.0, 0.0)
        picked.append((unpacked(all_branch[slot].astype(F32)) * alive).astype(BF16))
    down_t = down_t + dot_left_split(branch_map, jnp.concatenate(picked, axis=0))
    down_out[...] = down_t.T

    for copy in halos:
        copy.wait_send()
    all_copies(all_transfer, 0, NX).wait_send()
    all_copies(all_pairs, 1, NX).wait_send()
    all_copies(all_branch, 2, NZ).wait_send()
    all_copies(all_gram, 3, NY).wait_send()
    all_copies(all_share, 4, NY).wait_send()
    all_copies(all_ortho, 5, N_SUB, NX).wait_send()
    all_copies(all_branch, 6, 2 * NZ, NZ).wait_send()


def far_kernel(near, vt, down, out, total, sems):
    high = down[...].astype(BF16)
    low = (down[...] - high.astype(F32)).astype(BF16)
    copies = []
    for at in range(POINTS // FAR):
        columns = slice(at * FAR, (at + 1) * FAR)
        total[:, columns] = (
            near[:, columns] + dot_nn(high, vt[:, columns]) + dot_nn(low, vt[:, columns])
        )
        copies.append(
            pltpu.make_async_copy(total.at[:, columns], out.at[:, columns], sems.at[at])
        )
        copies[-1].start()
    for copy in copies:
        copy.wait()


def shards(
    sources,
    coords,
    leaf_basis,
    leaf_transfer,
    cluster_transfer,
    near_slots,
    near_count,
    cluster_partners,
    cluster_count,
    cluster_coupling,
    branch_partners,
    branch_count,
    branch_coupling_tiles,
):
    vmem = pl.BlockSpec(memory_space=pltpu.VMEM)
    smem = pl.BlockSpec(memory_space=pltpu.SMEM)
    hbm = pl.BlockSpec(memory_space=pltpu.HBM)
    near, vt, down = pl.pallas_call(
        main_kernel,
        out_shape=(
            jax.ShapeDtypeStruct((COLS, POINTS), F32),
            jax.ShapeDtypeStruct((RANK, POINTS), BF16),
            jax.ShapeDtypeStruct((COLS, RANK), F32),
        ),
        in_specs=[smem] * 2 + [hbm] * 11,
        out_specs=(vmem, vmem, vmem),
        scratch_shapes=[
            pltpu.VMEM((3, POINTS), BF16),
            pltpu.VMEM((HERE, RANK, LEAF), BF16),
            pltpu.VMEM((HERE, RANK, RANK), F32),
            pltpu.VMEM((1, RANK, RANK), F32),
            pltpu.SMEM((NEAR, HERE), jnp.int32),
            pltpu.SMEM((HERE,), jnp.int32),
            pltpu.SMEM((1, COUP), jnp.int32),
            pltpu.VMEM((1, COUP, RANK, RANK), F32),
            pltpu.SMEM((1, BCOUP), jnp.int32),
            pltpu.VMEM((1, BCOUP, RANK, RANK), F32),
            pltpu.VMEM((COLS, PADDED), BF16),
            pltpu.VMEM((FEAT, PADDED), BF16),
            pltpu.VMEM((FEAT, POINTS), BF16),
            pltpu.VMEM((PADDED, FEAT), BF16),
            pltpu.VMEM((NX, RANK // 2, 2 * RANK), BF16),
            pltpu.VMEM((NY, RANK // 2, 2 * RANK), BF16),
            pltpu.VMEM((NX, RANK, 2 * RANK), BF16),
            pltpu.VMEM((NY, RANK // 2, 2 * RANK), BF16),
            pltpu.VMEM((N_SUB, RANK // 2, 2 * RANK), BF16),
            pltpu.VMEM((N_BRANCH, RANK // 2, 2 * RANK), BF16),
            pltpu.VMEM((RANK, 128), F32),
            pltpu.VMEM((NEAR * LEAF, LEAF), BF16),
            pltpu.VMEM((NEAR * LEAF, LEAF), BF16),
            pltpu.SemaphoreType.DMA((14,)),
            pltpu.SemaphoreType.DMA((4,)),
            pltpu.SemaphoreType.DMA((4,)),
            pltpu.SemaphoreType.DMA((7,)),
            pltpu.SemaphoreType.DMA((7,)),
        ],
        compiler_params=pltpu.CompilerParams(
            collective_id=0, has_side_effects=True, vmem_limit_bytes=40 * 2**20
        ),
        name="h2_main",
    )(
        cluster_count,
        branch_count,
        *(
            pltpu.with_memory_space_constraint(operand, pltpu.HBM)
            for operand in (
                sources,
                coords,
                leaf_basis,
                leaf_transfer,
                cluster_transfer,
                near_slots.T,
                near_count,
                cluster_partners,
                cluster_coupling,
                branch_partners,
                branch_coupling_tiles,
            )
        )
    )
    return pl.pallas_call(
        far_kernel,
        out_shape=jax.ShapeDtypeStruct((COLS, POINTS), F32),
        in_specs=[vmem] * 3,
        out_specs=hbm,
        scratch_shapes=[
            pltpu.VMEM((COLS, POINTS), F32),
            pltpu.SemaphoreType.DMA((POINTS // FAR,)),
        ],
        compiler_params=pltpu.CompilerParams(vmem_limit_bytes=32 * 2**20),
        name="h2_far",
    )(near, vt, down)


def solution(mesh):
    return jax.shard_map(
        shards,
        mesh=mesh,
        in_specs=(
            P(None, ("branch", "sub")),
            P(None, ("branch", "sub")),
            P(("branch", "sub"), None, None),
            P(("branch", "sub"), None, None),
            P(("branch", "sub"), None, None),
            P(("branch", "sub"), None),
            P(("branch", "sub")),
            P(("branch", "sub"), None),
            P(("branch", "sub")),
            P(("branch", "sub"), None, None, None),
            P("branch", None),
            P("branch"),
            P("branch", None, None, None),
        ),
        out_specs=P(None, ("branch", "sub")),
        check_vma=False,
    )
```
